512 devices in a mesh: seq: 64 (over x, z), head: 8 (over y, core).
Axes of the slice: x: 4, y: 4, z: 16, core: 2. Of those that a mesh axis runs over, the one named last changes fastest.
Arguments:
- query_rows: bfloat16 [8192, 4096], P('seq', 'head'), may hold values from -2.5 to 2.5
- key_rows: bfloat16 [8192, 4096], P('seq', 'head'), may hold values from -2.5 to 2.5
- value_rows: bfloat16 [8192, 4096], P('seq', 'head'), may hold values from -6 to 6
- out_grad: bfloat16 [8192, 4096], P('seq', 'head'), may hold values from -6 to 6
- norm_gain: float32 [4096], P('head'), may hold values from 0.25 to 1.75
- decay_rate: float32 [32], P('head'), as said below
- doc_ids: int32 [8192], P('seq'), may hold values from 0 to 7, never falling along the last dimension, each value on 1 to 4096 neighbouring positions
Outputs:
- query_grad: bfloat16 [8192, 4096], P('seq', 'head')
- key_grad: bfloat16 [8192, 4096], P('seq', 'head')
- value_grad: bfloat16 [8192, 4096], P('seq', 'head')
The draws below stay inside these ranges and needn't reach their ends.
Inputs may be any that keep to these rules, and one draw needn't show every extreme that they name: `doc_ids`: document numbers never fall along the window; each of the 8 documents holds 1 to 4096 tokens, and one holds exactly 4096. `decay_rate`: every rate is positive and lies between 3 / 81920 and 1 / 30.
All inputs are finite; a program needn't handle non-finite values.
Results may differ from the reference program's by a relative error of at most 0.0063.
Values sent between devices are 32-bit elements; how exact they have to be, the bound alone decides.
No kernel may reach another device: no remote copies, remote signals or barrier semaphores. Data moves between devices by JAX's collectives and lax.ppermute only.
A program may use at most 128 MiB of HBM per device.

```python
import math
import jax
import jax.numpy as jnp
import numpy as np
from jax import lax

HEADS = 32
HEAD_DIM = 128
TOK_DEV = 128
DOCS = 8
SEQ = 8192


def draw_decay_rate(key, part):
    key = jax.random.fold_in(key, 7)
    slow_key, fast_key, pick_key = jax.random.split(key, 3)
    slow_rate = jnp.exp(jax.random.uniform(slow_key, (HEADS,), jnp.float32, math.log(0.3), math.log(3.0))) / SEQ
    fast_rate = jnp.exp(jax.random.uniform(fast_key, (HEADS,), jnp.float32, math.log(1.0 / 50.0), math.log(1.0 / 30.0)))
    fraction = 0.5
    chosen = jax.random.uniform(pick_key, (HEADS,), jnp.float32) < fraction
    return jnp.where(chosen, fast_rate, slow_rate).astype(jnp.float32)


def block_scale(stream_key, dims, cuts, least, largest):
    level, own = 1.0, jax.random.fold_in(stream_key, 6)
    for dim, parts in cuts:
        draws = jnp.exp(jax.random.uniform(jax.random.fold_in(own, dim), (parts,), jnp.float32, least / len(cuts), largest / len(cuts)))
        level = level * jnp.repeat(draws, dims[dim] // parts).reshape([-1 if axis == dim else 1 for axis in range(len(dims))])
    return level


def length_profile(number_of, total, bound, slope):
    portions = [(1 << 20) // math.isqrt(grade ** slope) + 1 for grade in range(2, number_of + 1)]
    spare, counts = total - bound - (number_of - 1), [1] * (number_of - 1)
    while spare > 0:
        free = [i for i in range(number_of - 1) if counts[i] < bound]
        pool, left = sum([portions[i] for i in free]), spare
        for i in free:
            addition = min(bound - counts[i], max(1, left * portions[i] // pool), spare)
            counts[i] = counts[i] + addition
            spare = spare - addition
    return np.array([bound] + counts)


def uneven(stream_key, count, total, reach, slope):
    if count == 2:
        one = jax.random.randint(stream_key, (), max(1, total - reach), min(reach, total - 1) + 1)
        return jnp.stack([one, total - one])
    sizes = jnp.asarray(length_profile(count, total, reach, slope), jnp.int32)
    pairs = (count - 1) // 2
    giver, taker = sizes[1:1 + 2 * pairs:2], sizes[2:2 + 2 * pairs:2]
    room = jnp.minimum(giver - 1, reach - taker)
    passed = jax.random.randint(jax.random.fold_in(stream_key, 1), (pairs,), 0, 1 << 20) % (room + 1)
    sizes = sizes.at[1:1 + 2 * pairs:2].set(giver - passed).at[2:2 + 2 * pairs:2].set(taker + passed)
    return sizes[jax.random.permutation(jax.random.fold_in(stream_key, 2), count)]


def centred(stream_key, extent, deviation, bound, shards=(), dtype=jnp.bfloat16):
    loudness = block_scale(stream_key, extent, shards, -0.22, 0.18) if shards else 1.0
    values = jax.random.normal(stream_key, extent, jnp.float32) * deviation * loudness
    return jnp.minimum(jnp.maximum(values, -bound), bound).astype(dtype)


def setup_inputs(seed: int = 0) -> dict:
    key_list = jax.random.split(jax.random.key(seed), 8)
    query_rows = centred(key_list[0], (SEQ, HEADS * HEAD_DIM), 0.3, 2.5, ((0, 64), (1, 8)))
    key_rows = centred(key_list[1], (SEQ, HEADS * HEAD_DIM), 0.3, 2.5, ((0, 64), (1, 8)))
    value_rows = centred(key_list[2], (SEQ, HEADS * HEAD_DIM), 1.0, 6.0, ((0, 64), (1, 8)))
    out_grad = centred(key_list[3], (SEQ, HEADS * HEAD_DIM), 1.0, 6.0, ((0, 64), (1, 8)))
    norm_gain = jnp.clip(1.0 + 0.15 * jax.random.normal(key_list[4], (HEADS * HEAD_DIM,), jnp.float32), 0.25, 1.75)
    decay_rate = draw_decay_rate(jax.random.fold_in(key_list[7], 71), 0)
    doc_ids = jnp.searchsorted(jnp.cumsum(uneven(key_list[6], DOCS, SEQ, SEQ // 2, 2)), jnp.arange(SEQ), side="right").astype(jnp.int32)
    return {"query_rows": query_rows, "key_rows": key_rows, "value_rows": value_rows, "out_grad": out_grad, "norm_gain": norm_gain, "decay_rate": decay_rate, "doc_ids": doc_ids}


epsilon = 1e-06

def as_float(values):
    return values.astype(jnp.float32)

def factors(docs, prev_doc, rates):
    block_len = docs.shape[0]
    position = jnp.arange(block_len).astype(jnp.float32)
    same_prev = docs == prev_doc
    same_last = docs == docs[block_len - 1]
    inflow = jnp.where(same_prev[:, None], jnp.exp(-rates[None, :] * (position[:, None] + 1.0)), 0.0)
    outflow = jnp.where(same_last[:, None], jnp.exp(-rates[None, :] * (block_len - 1.0 - position[:, None])), 0.0)
    passage = jnp.where(same_prev[block_len - 1], jnp.exp(-rates * block_len), 0.0)
    offset = position[:, None] - position[None, :]
    inside = (offset >= 0.0) & (docs[:, None] == docs[None, :])
    decays = jnp.where(inside[None], jnp.exp(-rates[:, None, None] * jnp.where(inside, offset, 0.0)[None]), 0.0)
    return (inflow, outflow, passage, decays)

def intra_weights(query_heads, key_heads, decays):
    scores = jnp.einsum('phd,uhd->hpu', as_float(query_heads), as_float(key_heads))
    return (scores * decays).astype(jnp.bfloat16)

def advance(carried, element):
    passage, local = element
    return (passage[:, None, None] * carried + local, carried)

def reference(query_rows, key_rows, value_rows, out_grad, norm_gain, decay_rate, doc_ids):
    blocks = SEQ // TOK_DEV
    width_all = HEADS * HEAD_DIM
    split_shape = (blocks, TOK_DEV, HEADS, HEAD_DIM)
    query_all = query_rows.reshape(split_shape)
    key_all = key_rows.reshape(split_shape)
    value_all = value_rows.reshape(split_shape)
    grad_all = out_grad.reshape(blocks, TOK_DEV, width_all)
    docs_all = doc_ids.reshape(blocks, TOK_DEV)
    prev_all = jnp.concatenate([jnp.full((1,), -1, jnp.int32), docs_all[:-1, TOK_DEV - 1].astype(jnp.int32)])

    def forward_part(inputs):
        key_heads, value_heads, docs, prev_doc = inputs
        inflow, outflow, passage, decays = factors(docs, prev_doc, decay_rate)
        key_out = (as_float(key_heads) * outflow[:, :, None]).astype(jnp.bfloat16)
        local_state = jnp.einsum('uhd,uhe->hde', as_float(key_out), as_float(value_heads))
        return (passage, local_state)
    passages, local_states = lax.map(forward_part, (key_all, value_all, docs_all, prev_all))
    zero_state = jnp.zeros((HEADS, HEAD_DIM, HEAD_DIM), jnp.float32)
    _, states_in = lax.scan(advance, zero_state, (passages, local_states))

    def middle_part(inputs):
        query_heads, key_heads, value_heads, grad_block, docs, prev_doc, state_full = inputs
        inflow, outflow, passage, decays = factors(docs, prev_doc, decay_rate)
        weights = intra_weights(query_heads, key_heads, decays)
        state_low = state_full.astype(jnp.bfloat16)
        attended = jnp.einsum('hpu,uhe->phe', as_float(weights), as_float(value_heads))
        attended = attended + inflow[:, :, None] * jnp.einsum('phd,hde->phe', as_float(query_heads), as_float(state_low))
        flat_out = attended.reshape(TOK_DEV, width_all)
        scaled = norm_gain[None, :] * as_float(grad_block)
        square_sum = lax.optimization_barrier(jnp.sum(flat_out * flat_out, axis=1))
        cross_sum = lax.optimization_barrier(jnp.sum(scaled * flat_out, axis=1))
        inv_rms = lax.rsqrt(square_sum / width_all + epsilon)
        grad_flat = scaled * inv_rms[:, None] - flat_out * (cross_sum * inv_rms ** 3 / width_all)[:, None]
        grad_heads = grad_flat.astype(jnp.bfloat16).reshape(TOK_DEV, HEADS, HEAD_DIM)
        query_in = (as_float(query_heads) * inflow[:, :, None]).astype(jnp.bfloat16)
        local_grad = jnp.einsum('phd,phe->hde', as_float(query_in), as_float(grad_heads))
        return (grad_heads, local_grad)
    grads_heads, local_grads = lax.map(middle_part, (query_all, key_all, value_all, grad_all, docs_all, prev_all, states_in))
    _, states_out = lax.scan(advance, zero_state, (passages, local_grads), reverse=True)

    def final_part(inputs):
        query_heads, key_heads, value_heads, grad_heads, docs, prev_doc, state_full, state_back = inputs
        inflow, outflow, passage, decays = factors(docs, prev_doc, decay_rate)
        weights = intra_weights(query_heads, key_heads, decays)
        state_low = as_float(state_full.astype(jnp.bfloat16))
        out_low = as_float(state_back.astype(jnp.bfloat16))
        grad_scores = jnp.einsum('phe,uhe->hpu', as_float(grad_heads), as_float(value_heads))
        grad_weights = as_float((grad_scores * decays).astype(jnp.bfloat16))
        query_grad = jnp.einsum('hpu,uhd->phd', grad_weights, as_float(key_heads))
        query_grad = query_grad + inflow[:, :, None] * jnp.einsum('phe,hde->phd', as_float(grad_heads), state_low)
        key_grad = jnp.einsum('hpu,phd->uhd', grad_weights, as_float(query_heads))
        key_grad = key_grad + outflow[:, :, None] * jnp.einsum('uhe,hde->uhd', as_float(value_heads), out_low)
        value_grad = jnp.einsum('hpu,phe->uhe', as_float(weights), as_float(grad_heads))
        value_grad = value_grad + outflow[:, :, None] * jnp.einsum('uhd,hde->uhe', as_float(key_heads), out_low)
        flat_shape = (TOK_DEV, width_all)
        return (query_grad.astype(jnp.bfloat16).reshape(flat_shape), key_grad.astype(jnp.bfloat16).reshape(flat_shape), value_grad.astype(jnp.bfloat16).reshape(flat_shape))
    query_grad, key_grad, value_grad = lax.map(final_part, (query_all, key_all, value_all, grads_heads, docs_all, prev_all, states_in, states_out))
    full_shape = (SEQ, width_all)
    return (query_grad.reshape(full_shape), key_grad.reshape(full_shape), value_grad.reshape(full_shape))
```

```python
import functools

import jax
import jax.numpy as jnp
from jax import lax
from jax.experimental import pallas as pl
from jax.experimental.pallas import tpu as pltpu
from jax.sharding import PartitionSpec as P

HEADS = 32
HEAD_DIM = 128
BLOCK = 128
LOCAL = 4
ROW = 16
ROWS = 4
PIECE = LOCAL * HEAD_DIM // ROW
PAD = 8

epsilon = 1e-06
f32 = jnp.float32
bf16 = jnp.bfloat16

VMEM = pl.BlockSpec(memory_space=pltpu.VMEM)
SMEM = pl.BlockSpec(memory_space=pltpu.SMEM)


def dot(a, b, a_dim, b_dim):
    return lax.dot_general(a, b, (((a_dim,), (b_dim,)), ((), ())), preferred_element_type=f32)


def square(row):
    return jnp.broadcast_to(row, (BLOCK, BLOCK))


def iota(axis):
    return lax.broadcasted_iota(jnp.int32, (BLOCK, BLOCK), axis).astype(f32)


def head(h):
    return slice(h * HEAD_DIM, (h + 1) * HEAD_DIM)


def outflow_of(doc_col, doc_row, rate):
    last = doc_row[:, BLOCK - 1 :]
    return jnp.where(doc_col == last, jnp.exp(-rate * (BLOCK - 1.0 - iota(0))), 0.0)


def inflow_of(doc_col, prev, rate):
    return jnp.where(doc_col == prev, jnp.exp(-rate * (iota(0) + 1.0)), 0.0)


def decays_of(doc_col, doc_row, rate):
    offset = iota(0) - iota(1)
    inside = (offset >= 0.0) & (doc_col == doc_row)
    return jnp.where(inside, jnp.exp(-rate * jnp.maximum(offset, 0.0)), 0.0)


def docs_of(docs):
    row = docs[...].astype(f32)
    wide = square(row)
    return wide.T, wide


def put_pieces(out, h, matrix):
    each = ROW // LOCAL
    for i in range(each):
        out[h * each + i, 0:PIECE, :] = matrix[i * PIECE : (i + 1) * PIECE]


def get_pieces(pieces, h):
    each = ROW // LOCAL
    return jnp.concatenate([pieces[h * each + i, 0:PIECE, :] for i in range(each)], axis=0)


def local_state_kernel(rates, docs, key, value, out):
    doc_col, doc_row = docs_of(docs)
    for h in range(LOCAL):
        outflow = outflow_of(doc_col, doc_row, rates[h])
        key_out = (key[:, head(h)].astype(f32) * outflow).astype(bf16)
        put_pieces(out, h, dot(key_out, value[:, head(h)], 0, 0))
    last = jnp.broadcast_to(doc_row[0:PAD, BLOCK - 1 :], (PAD, BLOCK))
    for i in range(ROW):
        out[i, PIECE:, :] = last


def intra_kernel(rates, docs, query, key, value, weights, attended):
    doc_col, doc_row = docs_of(docs)
    for h in range(LOCAL):
        scores = dot(query[:, head(h)], key[:, head(h)], 1, 1)
        low = (scores * decays_of(doc_col, doc_row, rates[h])).astype(bf16)
        weights[h] = low
        attended[:, head(h)] = dot(low, value[:, head(h)], 1, 0)


def my_place():
    place = lax.axis_index("seq")
    return place // ROW, place % ROW


def my_rate(rates):
    return rates[my_place()[1] // (ROW // LOCAL)]


def faded(rate, blocks):
    return jnp.exp(jnp.full((1, BLOCK), -BLOCK * blocks, f32) * rate)


def row_total_kernel(rates, pieces, out):
    fade = faded(my_rate(rates), 1.0)
    total = pieces[0, 0:PIECE, :]
    for z in range(1, ROW):
        same = pieces[z, PIECE : PIECE + 1, :] == pieces[z - 1, PIECE : PIECE + 1, :]
        total = jnp.where(same, fade, 0.0) * total + pieces[z, 0:PIECE, :]
    for x in range(ROWS):
        out[x, 0:PIECE, :] = total
        out[x, PIECE:, :] = pieces[ROW - 1, PIECE:, :]


def row_scan_kernel(rates, pieces, totals, out):
    rate, (mine, _) = my_rate(rates), my_place()
    fade = faded(rate, 1.0)
    before = jnp.maximum(mine - 1, 0)
    prev = totals[before, PIECE:, :]
    state = jnp.zeros((PIECE, BLOCK), f32)
    for x in range(ROWS - 1):
        same = (totals[x, PIECE : PIECE + 1, :] == prev[0:1]) & (x < mine)
        gap = jnp.maximum(mine - 1 - x, 0).astype(f32) * ROW
        state = state + jnp.where(same, faded(rate, gap), 0.0) * totals[x, 0:PIECE, :]
    prev = jnp.where(mine > 0, prev, -1.0)
    for z in range(ROW):
        out[z, 0:PIECE, :] = state
        out[z, PIECE:, :] = prev
        last = pieces[z, PIECE:, :]
        state = jnp.where(last[0:1] == prev[0:1], fade, 0.0) * state + pieces[z, 0:PIECE, :]
        prev = last


def attend_kernel(rates, docs, gain, query, grad, intra, states, attended, sums):
    doc_col, _ = docs_of(docs)
    prev = states[0, PIECE : PIECE + 1, :]
    squares = jnp.zeros((BLOCK, BLOCK), f32)
    crosses = jnp.zeros((BLOCK, BLOCK), f32)
    for h in range(LOCAL):
        low = get_pieces(states, h).astype(bf16)
        inflow = inflow_of(doc_col, prev, rates[h])
        both = intra[:, head(h)] + inflow * dot(query[:, head(h)], low, 1, 0)
        attended[:, head(h)] = both
        squares = squares + both * both
        crosses = crosses + gain[:, head(h)] * grad[:, head(h)].astype(f32) * both
    square_row = jnp.sum(squares.T, axis=0, keepdims=True)
    cross_row = jnp.sum(crosses.T, axis=0, keepdims=True)
    for i in range(sums.shape[0]):
        sums[i, 0:1, :] = square_row
        sums[i, 1:2, :] = cross_row


def grad_kernel(rates, docs, gain, query, grad, attended, states, sums, low_grad, out):
    doc_col, _ = docs_of(docs)
    prev = states[0, PIECE : PIECE + 1, :]
    both = jnp.sum(sums[...], axis=0)
    width = HEADS * HEAD_DIM
    inv_rms = lax.rsqrt(both[0:1] / width + epsilon)
    slope = both[1:2] * (inv_rms * inv_rms * inv_rms) / width
    inv_col, slope_col = square(inv_rms).T, square(slope).T
    for h in range(LOCAL):
        scaled = gain[:, head(h)] * grad[:, head(h)].astype(f32)
        low = (scaled * inv_col - attended[:, head(h)] * slope_col).astype(bf16)
        low_grad[:, head(h)] = low
        inflow = inflow_of(doc_col, prev, rates[h])
        query_in = (query[:, head(h)].astype(f32) * inflow).astype(bf16)
        put_pieces(out, h, dot(query_in, low, 0, 0))


def back_intra_kernel(
    rates, docs, query, key, value, weights, low_grad, states, query_grad, key_part, value_part
):
    doc_col, doc_row = docs_of(docs)
    prev = states[0, PIECE : PIECE + 1, :]
    for h in range(LOCAL):
        low = low_grad[:, head(h)]
        scores = dot(low, value[:, head(h)], 1, 1)
        grad_weights = (scores * decays_of(doc_col, doc_row, rates[h])).astype(bf16)
        state = get_pieces(states, h).astype(bf16)
        inflow = inflow_of(doc_col, prev, rates[h])
        whole = dot(grad_weights, key[:, head(h)], 1, 0) + inflow * dot(low, state, 1, 1)
        query_grad[:, head(h)] = whole.astype(bf16)
        key_part[:, head(h)] = dot(grad_weights, query[:, head(h)], 0, 0)
        value_part[:, head(h)] = dot(weights[h], low, 0, 0)


def back_total_kernel(rates, pieces, totals, grads, out):
    fade = faded(my_rate(rates), 1.0)
    total = grads[ROW - 1]
    mine, _ = my_place()
    before = totals[jnp.maximum(mine - 1, 0), PIECE : PIECE + 1, :]
    before = jnp.where(mine > 0, before, -1.0)
    for z in range(ROW - 2, -1, -1):
        older = pieces[z - 1, PIECE : PIECE + 1, :] if z else before
        same = pieces[z, PIECE : PIECE + 1, :] == older
        total = jnp.where(same, fade, 0.0) * total + grads[z]
    for x in range(ROWS):
        out[x] = total


def back_scan_kernel(rates, pieces, totals, grads, later, out):
    rate, (mine, _) = my_rate(rates), my_place()
    fade = faded(rate, 1.0)
    here = pieces[ROW - 1, PIECE : PIECE + 1, :]
    state = jnp.zeros((PIECE, BLOCK), f32)
    for x in range(1, ROWS):
        same = (totals[x - 1, PIECE : PIECE + 1, :] == here) & (x > mine)
        gap = jnp.maximum(x - 1 - mine, 0).astype(f32) * ROW
        state = state + jnp.where(same, faded(rate, gap), 0.0) * later[x]
    for z in range(ROW - 1, -1, -1):
        out[z] = state
        if z:
            same = pieces[z, PIECE : PIECE + 1, :] == pieces[z - 1, PIECE : PIECE + 1, :]
            state = jnp.where(same, fade, 0.0) * state + grads[z]


def finish_kernel(rates, docs, key, value, key_part, value_part, states, key_grad, value_grad):
    doc_col, doc_row = docs_of(docs)
    for h in range(LOCAL):
        low = get_pieces(states, h).astype(bf16)
        outflow = outflow_of(doc_col, doc_row, rates[h])
        more = outflow * dot(value[:, head(h)], low, 1, 1)
        key_grad[:, head(h)] = (key_part[:, head(h)] + more).astype(bf16)
        more = outflow * dot(key[:, head(h)], low, 1, 0)
        value_grad[:, head(h)] = (value_part[:, head(h)] + more).astype(bf16)


def call(kernel, name, outs, *args, flops=1):
    shapes = [jax.ShapeDtypeStruct(shape, dtype) for shape, dtype in outs]
    moved = sum(a.size * a.dtype.itemsize for a in (*args, *shapes))
    out = pl.pallas_call(
        kernel,
        out_shape=shapes,
        in_specs=[SMEM] + [VMEM] * (len(args) - 1),
        out_specs=[VMEM] * len(shapes),
        name=name,
        compiler_params=pltpu.CompilerParams(vmem_limit_bytes=32 * 1024 * 1024),
        cost_estimate=pl.CostEstimate(flops=flops, bytes_accessed=moved, transcendentals=0),
    )(*args)
    return out[0] if len(out) == 1 else out


def per_device(query, key, value, grad, gain, rates, doc_ids):
    along = [[x * ROW + z for z in range(ROW)] for x in range(ROWS)]
    across = [[x * ROW + z for x in range(ROWS)] for z in range(ROW)]
    swap_z = functools.partial(
        lax.all_to_all, axis_name="seq", split_axis=0, concat_axis=0, axis_index_groups=along, tiled=True
    )
    swap_x = functools.partial(
        lax.all_to_all, axis_name="seq", split_axis=0, concat_axis=0, axis_index_groups=across, tiled=True
    )
    docs = doc_ids.reshape(1, BLOCK)
    gain = gain.reshape(1, LOCAL * HEAD_DIM)
    wide = (BLOCK, LOCAL * HEAD_DIM)
    tall = (PIECE + PAD, BLOCK)
    one = 2 * LOCAL * BLOCK * BLOCK * HEAD_DIM

    local = call(local_state_kernel, "local_state", [((ROW, *tall), f32)], rates, docs, key, value, flops=one)
    pieces = swap_z(local)
    weights, intra = call(
        intra_kernel, "intra", [((LOCAL, BLOCK, BLOCK), bf16), (wide, f32)], rates, docs, query, key, value, flops=2 * one
    )
    total = call(row_total_kernel, "row_total", [((ROWS, *tall), f32)], rates, pieces)
    totals = swap_x(total)
    scanned = call(row_scan_kernel, "row_scan", [((ROW, *tall), f32)], rates, pieces, totals)
    states = swap_z(scanned)
    attended, sums = call(
        attend_kernel, "attend", [(wide, f32), ((8, 2, BLOCK), f32)], rates, docs, gain, query, grad, intra, states, flops=one
    )
    sums = lax.all_to_all(sums, "head", 0, 0, tiled=True)
    low_grad, local_grad = call(
        grad_kernel, "grad", [(wide, bf16), ((ROW, PIECE, BLOCK), f32)],
        rates, docs, gain, query, grad, attended, states, sums, flops=one,
    )
    grads = swap_z(local_grad)
    query_grad, key_part, value_part = call(
        back_intra_kernel, "back_intra", [(wide, bf16), (wide, f32), (wide, f32)],
        rates, docs, query, key, value, weights, low_grad, states, flops=5 * one,
    )
    back_total = call(back_total_kernel, "back_total", [((ROWS, PIECE, BLOCK), f32)], rates, pieces, totals, grads)
    later = swap_x(back_total)
    back = call(back_scan_kernel, "back_scan", [((ROW, PIECE, BLOCK), f32)], rates, pieces, totals, grads, later)
    states_out = swap_z(back)
    key_grad, value_grad = call(
        finish_kernel, "finish", [(wide, bf16), (wide, bf16)],
        rates, docs, key, value, key_part, value_part, states_out, flops=2 * one,
    )
    return query_grad, key_grad, value_grad


def solution(mesh):
    return jax.shard_map(
        per_device,
        mesh=mesh,
        in_specs=(
            P("seq", "head"),
            P("seq", "head"),
            P("seq", "head"),
            P("seq", "head"),
            P("head"),
            P("head"),
            P("seq"),
        ),
        out_specs=(P("seq", "head"), P("seq", "head"), P("seq", "head")),
        check_vma=False,
    )
```

```python
import functools

import jax
import jax.numpy as jnp
from jax import lax
from jax.experimental import pallas as pl
from jax.experimental.pallas import tpu as pltpu
from jax.sharding import PartitionSpec as P

HEADS = 32
HEAD_DIM = 128
BLOCK = 128
LOCAL = 4
GROUPS = 4
ROWS = 4
HEAD_PARTS = 8
DOC = HEAD_DIM
TALL = HEAD_DIM + 8

epsilon = 1e-06
f32 = jnp.float32
bf16 = jnp.bfloat16

VMEM = pl.BlockSpec(memory_space=pltpu.VMEM)
SMEM = pl.BlockSpec(memory_space=pltpu.SMEM)


def dot(a, b, a_dim, b_dim):
    return lax.dot_general(a, b, (((a_dim,), (b_dim,)), ((), ())), preferred_element_type=f32)


def square(row):
    return jnp.broadcast_to(row, (BLOCK, BLOCK))


def iota(axis):
    return lax.broadcasted_iota(jnp.int32, (BLOCK, BLOCK), axis).astype(f32)


def head(h):
    start = h * HEAD_DIM
    if not isinstance(h, int):
        start = pl.multiple_of(start, HEAD_DIM)
    return pl.ds(start, HEAD_DIM)


def outflow_of(doc_row, rate):
    doc_col = square(doc_row).T
    last = doc_row[:, BLOCK - 1 :]
    return jnp.where(doc_col == last, jnp.exp(-rate * (BLOCK - 1.0 - iota(0))), 0.0)


def inflow_of(doc_row, rate):
    doc_col = square(doc_row).T
    return jnp.where(doc_col == doc_row[:, 0:1], jnp.exp(-rate * (iota(0) + 1.0)), 0.0)


def decays_of(doc_row, rate):
    doc_col = square(doc_row).T
    offset = iota(0) - iota(1)
    inside = (offset >= 0.0) & (doc_col == doc_row)
    return jnp.where(inside, jnp.exp(-rate * jnp.maximum(offset, 0.0)), 0.0)


def place():
    mine = lax.axis_index("seq")
    return mine // (GROUPS * LOCAL), (mine // LOCAL) % GROUPS, mine % LOCAL


def faded(rate, blocks):
    return jnp.exp(jnp.full((1, BLOCK), -BLOCK * blocks, f32) * rate)


def passing(same, fade):
    return jnp.where(same, fade, 0.0)


def first_doc(pieces, i):
    return jnp.broadcast_to(pieces[i, DOC : DOC + 1, 0:1], (1, BLOCK))


def last_doc(pieces, i):
    return jnp.broadcast_to(pieces[i, DOC : DOC + 1, BLOCK - 1 :], (1, BLOCK))


def row_doc(row, k):
    return row[k, DOC : DOC + 1, :]


def before_row(x, earlier):
    return jnp.where(x > 0, earlier[DOC : DOC + 1, :], -1.0)


def before_group(x, k, row, earlier):
    inside = row_doc(row, jnp.maximum(k - 1, 0))
    return jnp.where(k > 0, inside, before_row(x, earlier))


def local_state_kernel(rates, docs, key, value, out):
    doc_row = docs[...].astype(f32)
    for h in range(LOCAL):
        key_out = (key[:, head(h)].astype(f32) * outflow_of(doc_row, rates[h])).astype(bf16)
        out[h, 0:HEAD_DIM, :] = dot(key_out, value[:, head(h)], 0, 0)
        out[h, DOC:, :] = jnp.broadcast_to(doc_row, (TALL - DOC, BLOCK))


def intra_kernel(rates, docs, gain, query, key, value, grad, weights, *outs):
    doc_row = docs[...].astype(f32)
    member = place()[2]
    for d in range(LOCAL):
        h = member ^ d
        scores = dot(query[:, head(h)], key[:, head(h)], 1, 1)
        low = (scores * decays_of(doc_row, rates[h])).astype(bf16)
        weights[d] = low
        outs[d][0] = dot(low, value[:, head(h)], 1, 0)
        outs[d][1] = query[:, head(h)].astype(f32)
        outs[d][2] = gain[:, head(h)] * grad[:, head(h)].astype(f32)


def back_intra_kernel(
    rates, docs, query, key, value, weights, in0, in1, in2, in3, query_grad, key_part, value_part
):
    doc_row = docs[...].astype(f32)
    member = place()[2]
    for d, piece in enumerate((in0, in1, in2, in3)):
        h = member ^ d
        low = piece[0].astype(bf16)
        scores = dot(low, value[:, head(h)], 1, 1)
        grad_weights = (scores * decays_of(doc_row, rates[h])).astype(bf16)
        whole = dot(grad_weights, key[:, head(h)], 1, 0) + piece[1]
        query_grad[:, head(h)] = whole.astype(bf16)
        key_part[:, head(h)] = dot(grad_weights, query[:, head(h)], 0, 0)
        value_part[:, head(h)] = dot(weights[d], low, 0, 0)


def finish_kernel(rates, docs, key, value, key_part, value_part, states, key_grad, value_grad):
    doc_row = docs[...].astype(f32)
    for h in range(LOCAL):
        low = states[h].astype(bf16)
        outflow = outflow_of(doc_row, rates[h])
        more = outflow * dot(value[:, head(h)], low, 1, 1)
        key_grad[:, head(h)] = (key_part[:, head(h)] + more).astype(bf16)
        more = outflow * dot(key[:, head(h)], low, 1, 0)
        value_grad[:, head(h)] = (value_part[:, head(h)] + more).astype(bf16)


def group_total_kernel(rates, pieces, out):
    fade = faded(rates[place()[2]], 1.0)
    total = pieces[0, 0:HEAD_DIM, :]
    for i in range(1, LOCAL):
        same = last_doc(pieces, i) == last_doc(pieces, i - 1)
        total = passing(same, fade) * total + pieces[i, 0:HEAD_DIM, :]
    last = jnp.broadcast_to(last_doc(pieces, LOCAL - 1), (TALL - DOC, BLOCK))
    for k in range(GROUPS):
        out[k, 0:HEAD_DIM, :] = total
        out[k, DOC:, :] = last


def row_total_kernel(rates, row, out):
    fade = faded(rates[place()[2]], 1.0 * LOCAL)
    total = row[0, 0:HEAD_DIM, :]
    for k in range(1, GROUPS):
        same = row_doc(row, k) == row_doc(row, k - 1)
        total = passing(same, fade) * total + row[k, 0:HEAD_DIM, :]
    out[0:HEAD_DIM, :] = total
    out[DOC:, :] = row[GROUPS - 1, DOC:, :]


def attend_kernel(
    rates, pieces, row, near, far, in0, in1, in2, in3, attended, state_low, sums
):
    x, group, member = place()
    rate = rates[member]
    prev = before_row(x, near)
    same = (far[DOC : DOC + 1, :] == prev) & (x > 1)
    state = near[0:HEAD_DIM, :] + passing(same, faded(rate, 16.0)) * far[0:HEAD_DIM, :]
    for k in range(GROUPS - 1):
        last = row_doc(row, k)
        longer = passing(last == prev, faded(rate, 1.0 * LOCAL)) * state + row[k, 0:HEAD_DIM, :]
        state = jnp.where(k < group, longer, state)
        prev = jnp.where(k < group, last, prev)
    for i in range(LOCAL):
        low = passing(first_doc(pieces, i) == prev, 1.0) * state
        state_low[i] = low.astype(bf16)
        last = last_doc(pieces, i)
        if i < LOCAL - 1:
            state = passing(last == prev, faded(rate, 1.0)) * state + pieces[i, 0:HEAD_DIM, :]
        prev = last
    line = lax.broadcasted_iota(jnp.int32, (2 * LOCAL, BLOCK), 0)
    both = jnp.zeros((2 * LOCAL, BLOCK), f32)
    for d, piece in enumerate((in0, in1, in2, in3)):
        i = member ^ d
        inflow = inflow_of(pieces[i, DOC : DOC + 1, :], rate)
        whole = piece[0] + inflow * dot(piece[1].astype(bf16), state_low[i], 1, 0)
        attended[d] = whole
        squares = jnp.sum((whole * whole).T, axis=0, keepdims=True)
        crosses = jnp.sum((whole * piece[2]).T, axis=0, keepdims=True)
        both = both + jnp.where(line == i, squares, 0.0) + jnp.where(line == LOCAL + i, crosses, 0.0)
    for j in range(sums.shape[0]):
        sums[j] = both


def grad_kernel(
    rates, pieces, row, near, in0, in1, in2, in3, attended, state_low, sums, *outs
):
    x, group, member = place()
    rate = rates[member]
    both = jnp.sum(sums[...], axis=0)
    line = lax.broadcasted_iota(jnp.int32, (2 * LOCAL, BLOCK), 0)
    width = HEADS * HEAD_DIM
    local_grads, totals = outs[LOCAL:]
    for d, piece in enumerate((in0, in1, in2, in3)):
        i = member ^ d
        square_sum = jnp.sum(jnp.where(line == i, both, 0.0), axis=0, keepdims=True)
        cross_sum = jnp.sum(jnp.where(line == LOCAL + i, both, 0.0), axis=0, keepdims=True)
        inv_rms = lax.rsqrt(square_sum / width + epsilon)
        slope = cross_sum * (inv_rms * inv_rms * inv_rms) / width
        low = (piece[2] * square(inv_rms).T - attended[d] * square(slope).T).astype(bf16)
        inflow = inflow_of(pieces[i, DOC : DOC + 1, :], rate)
        outs[d][0] = low.astype(f32)
        outs[d][1] = inflow * dot(low, state_low[i], 1, 1)
        local_grads[i] = dot((piece[1] * inflow).astype(bf16), low, 0, 0)
    prev = before_group(x, group, row, near)
    fade = faded(rate, 1.0)
    total = jnp.zeros((HEAD_DIM, HEAD_DIM), f32)
    for i in range(LOCAL - 1, -1, -1):
        older = last_doc(pieces, i - 1) if i else prev
        mine = passing(first_doc(pieces, i) == older, 1.0) * local_grads[i]
        local_grads[i] = mine
        total = passing(last_doc(pieces, i) == older, fade) * total + mine
    for k in range(GROUPS):
        totals[k] = total


def back_row_kernel(rates, row, near, grads, out):
    x, _, member = place()
    fade = faded(rates[member], 1.0 * LOCAL)
    total = grads[GROUPS - 1]
    for k in range(GROUPS - 2, -1, -1):
        older = row_doc(row, k - 1) if k else before_row(x, near)
        total = passing(row_doc(row, k) == older, fade) * total + grads[k]
    out[0:HEAD_DIM, :] = total
    out[DOC:, :] = row[GROUPS - 1, DOC:, :]


def back_state_kernel(rates, pieces, row, grads, near, far, local_grads, out):
    x, group, member = place()
    rate = rates[member]
    same = (near[DOC : DOC + 1, :] == row_doc(row, GROUPS - 1)) & (x < ROWS - 2)
    state = near[0:HEAD_DIM, :] + passing(same, faded(rate, 16.0)) * far[0:HEAD_DIM, :]
    for k in range(GROUPS - 1, 0, -1):
        same = row_doc(row, k) == row_doc(row, k - 1)
        longer = passing(same, faded(rate, 1.0 * LOCAL)) * state + grads[k]
        state = jnp.where(k > group, longer, state)
    for i in range(LOCAL - 1, -1, -1):
        out[i] = state
        if i:
            same = last_doc(pieces, i) == last_doc(pieces, i - 1)
            state = passing(same, faded(rate, 1.0)) * state + local_grads[i]


def call(kernel, name, outs, *args, flops=1):
    shapes = [jax.ShapeDtypeStruct(shape, dtype) for shape, dtype in outs]
    moved = sum(a.size * a.dtype.itemsize for a in (*args, *shapes))
    out = pl.pallas_call(
        kernel,
        out_shape=shapes,
        in_specs=[SMEM] + [VMEM] * (len(args) - 1),
        out_specs=[VMEM] * len(shapes),
        name=name,
        compiler_params=pltpu.CompilerParams(vmem_limit_bytes=32 * 1024 * 1024),
        cost_estimate=pl.CostEstimate(flops=flops, bytes_accessed=moved, transcendentals=0),
    )(*args)
    return out[0] if len(out) == 1 else out


def per_device(query, key, value, grad, gain, rates, doc_ids):
    row_len = GROUPS * LOCAL
    blocks = range(ROWS * row_len)
    near_groups = [[i + j for j in range(LOCAL)] for i in blocks if i % LOCAL == 0]
    far_groups = [
        [x * row_len + k * LOCAL + j for k in range(GROUPS)] for x in range(ROWS) for j in range(LOCAL)
    ]
    sum_groups = [[i * HEAD_PARTS + h for i in near for h in range(HEAD_PARTS)] for near in near_groups]
    swap = functools.partial(lax.all_to_all, axis_name="seq", split_axis=0, concat_axis=0, tiled=True)

    def partner(piece, d):
        return lax.ppermute(piece, "seq", [(i, i ^ d) for i in blocks]) if d else piece

    def to_row(piece, by):
        pairs = [(i, i + by * row_len) for i in blocks if 0 <= i + by * row_len < len(blocks)]
        return lax.ppermute(piece, "seq", pairs)

    docs = doc_ids.reshape(1, BLOCK)
    gain = gain.reshape(1, LOCAL * HEAD_DIM)
    wide = (BLOCK, LOCAL * HEAD_DIM)
    tall = (TALL, HEAD_DIM)
    mat = (BLOCK, HEAD_DIM)
    one = 2 * LOCAL * BLOCK * BLOCK * HEAD_DIM

    local = call(local_state_kernel, "local_state", [((LOCAL, *tall), f32)], rates, docs, key, value, flops=one)
    pieces = swap(local, axis_index_groups=near_groups)
    total = call(group_total_kernel, "group_total", [((GROUPS, *tall), f32)], rates, pieces)
    row = swap(total, axis_index_groups=far_groups)
    weights, *sent = call(
        intra_kernel, "intra", [((LOCAL, *mat), bf16)] + [((3, *mat), f32)] * LOCAL,
        rates, docs, gain, query, key, value, grad, flops=2 * one,
    )
    tokens = [partner(piece, d) for d, piece in enumerate(sent)]
    row_total = call(row_total_kernel, "row_total", [(tall, f32)], rates, row)
    near, far = to_row(row_total, 1), to_row(row_total, 2)
    attended, state_low, sums = call(
        attend_kernel, "attend",
        [((LOCAL, *mat), f32), ((LOCAL, *mat), bf16), ((LOCAL * HEAD_PARTS, 2 * LOCAL, BLOCK), f32)],
        rates, pieces, row, near, far, *tokens, flops=one,
    )
    sums = lax.all_to_all(sums, ("seq", "head"), 0, 0, axis_index_groups=sum_groups, tiled=True)
    *sent, local_grads, totals = call(
        grad_kernel, "grad", [((2, *mat), f32)] * LOCAL + [((LOCAL, *mat), f32), ((GROUPS, *mat), f32)],
        rates, pieces, row, near, *tokens, attended, state_low, sums, flops=2 * one,
    )
    row_grads = swap(totals, axis_index_groups=far_groups)
    back = [partner(piece, d) for d, piece in enumerate(sent)]
    query_grad, key_part, value_part = call(
        back_intra_kernel, "back_intra", [(wide, bf16), (wide, f32), (wide, f32)],
        rates, docs, query, key, value, weights, *back, flops=4 * one,
    )
    back_total = call(back_row_kernel, "back_row", [(tall, f32)], rates, row, near, row_grads)
    later, latest = to_row(back_total, -1), to_row(back_total, -2)
    states = call(
        back_state_kernel, "back_state", [((LOCAL, *mat), f32)],
        rates, pieces, row, row_grads, later, latest, local_grads,
    )
    states, key_part, value_part = lax.optimization_barrier((states, key_part, value_part))
    states = swap(states, axis_index_groups=near_groups)
    key_grad, value_grad = call(
        finish_kernel, "finish", [(wide, bf16), (wide, bf16)],
        rates, docs, key, value, key_part, value_part, states, flops=2 * one,
    )
    return query_grad, key_grad, value_grad


def solution(mesh):
    return jax.shard_map(
        per_device,
        mesh=mesh,
        in_specs=(
            P("seq", "head"),
            P("seq", "head"),
            P("seq", "head"),
            P("seq", "head"),
            P("head"),
            P("head"),
            P("seq"),
        ),
        out_specs=(P("seq", "head"), P("seq", "head"), P("seq", "head")),
        check_vma=False,
    )
```

```python
import functools

import jax
import jax.numpy as jnp
from jax import lax
from jax.experimental import pallas as pl
from jax.experimental.pallas import tpu as pltpu
from jax.sharding import PartitionSpec as P

HEADS = 32
HEAD_DIM = 128
BLOCK = 128
LOCAL = 4
MEMBERS = 4
GROUPS = 4
ROWS = 4
OWNERS = ROWS * MEMBERS
PIECE = LOCAL * HEAD_DIM // OWNERS
PAD = 8
DOC = ROWS * PIECE
TALL = DOC + 8

epsilon = 1e-06
f32 = jnp.float32
bf16 = jnp.bfloat16

VMEM = pl.BlockSpec(memory_space=pltpu.VMEM)
SMEM = pl.BlockSpec(memory_space=pltpu.SMEM)


def dot(a, b, a_dim, b_dim):
    return lax.dot_general(a, b, (((a_dim,), (b_dim,)), ((), ())), preferred_element_type=f32)


def square(row):
    return jnp.broadcast_to(row, (BLOCK, BLOCK))


def iota(axis):
    return lax.broadcasted_iota(jnp.int32, (BLOCK, BLOCK), axis).astype(f32)


def head(h):
    return slice(h * HEAD_DIM, (h + 1) * HEAD_DIM)


def outflow_of(doc_col, doc_row, rate):
    last = doc_row[:, BLOCK - 1 :]
    return jnp.where(doc_col == last, jnp.exp(-rate * (BLOCK - 1.0 - iota(0))), 0.0)


def inflow_of(doc_col, doc_row, rate):
    return jnp.where(doc_col == doc_row[:, 0:1], jnp.exp(-rate * (iota(0) + 1.0)), 0.0)


def decays_of(doc_col, doc_row, rate):
    offset = iota(0) - iota(1)
    inside = (offset >= 0.0) & (doc_col == doc_row)
    return jnp.where(inside, jnp.exp(-rate * jnp.maximum(offset, 0.0)), 0.0)


def docs_of(docs):
    row = docs[...].astype(f32)
    return square(row).T, row


def put_pieces(out, h, matrix):
    each = OWNERS // LOCAL
    for i in range(each):
        out[h * each + i, 0:PIECE, :] = matrix[i * PIECE : (i + 1) * PIECE]


def get_pieces(pieces, h):
    each = OWNERS // LOCAL
    return jnp.concatenate([pieces[h * each + i] for i in range(each)], axis=0)


def local_state_kernel(rates, docs, key, value, out):
    doc_col, doc_row = docs_of(docs)
    for h in range(LOCAL):
        outflow = outflow_of(doc_col, doc_row, rates[h])
        key_out = (key[:, head(h)].astype(f32) * outflow).astype(bf16)
        put_pieces(out, h, dot(key_out, value[:, head(h)], 0, 0))
    for i in range(OWNERS):
        out[i, PIECE:, :] = jnp.broadcast_to(doc_row, (PAD, BLOCK))


def intra_kernel(rates, docs, query, key, value, weights, attended):
    doc_col, doc_row = docs_of(docs)
    for h in range(LOCAL):
        scores = dot(query[:, head(h)], key[:, head(h)], 1, 1)
        low = (scores * decays_of(doc_col, doc_row, rates[h])).astype(bf16)
        weights[h] = low
        attended[:, head(h)] = dot(low, value[:, head(h)], 1, 0)


def attend_kernel(rates, docs, gain, query, grad, intra, states, attended, sums):
    doc_col, doc_row = docs_of(docs)
    squares = jnp.zeros((BLOCK, BLOCK), f32)
    crosses = jnp.zeros((BLOCK, BLOCK), f32)
    for h in range(LOCAL):
        low = get_pieces(states, h).astype(bf16)
        inflow = inflow_of(doc_col, doc_row, rates[h])
        whole = intra[:, head(h)] + inflow * dot(query[:, head(h)], low, 1, 0)
        attended[:, head(h)] = whole
        squares = squares + whole * whole
        crosses = crosses + gain[:, head(h)] * grad[:, head(h)].astype(f32) * whole
    square_row = jnp.sum(squares.T, axis=0, keepdims=True)
    cross_row = jnp.sum(crosses.T, axis=0, keepdims=True)
    for i in range(sums.shape[0]):
        sums[i, 0:1, :] = square_row
        sums[i, 1:2, :] = cross_row


def grad_kernel(rates, docs, gain, query, grad, attended, sums, low_grad, out):
    doc_col, doc_row = docs_of(docs)
    both = jnp.sum(sums[...], axis=0)
    width = HEADS * HEAD_DIM
    inv_rms = lax.rsqrt(both[0:1] / width + epsilon)
    slope = both[1:2] * (inv_rms * inv_rms * inv_rms) / width
    inv_col, slope_col = square(inv_rms).T, square(slope).T
    for h in range(LOCAL):
        scaled = gain[:, head(h)] * grad[:, head(h)].astype(f32)
        low = (scaled * inv_col - attended[:, head(h)] * slope_col).astype(bf16)
        low_grad[:, head(h)] = low
        inflow = inflow_of(doc_col, doc_row, rates[h])
        query_in = (query[:, head(h)].astype(f32) * inflow).astype(bf16)
        put_pieces(out, h, dot(query_in, low, 0, 0))


def back_intra_kernel(
    rates, docs, query, key, value, weights, low_grad, states, query_grad, key_part, value_part
):
    doc_col, doc_row = docs_of(docs)
    for h in range(LOCAL):
        low = low_grad[:, head(h)]
        scores = dot(low, value[:, head(h)], 1, 1)
        grad_weights = (scores * decays_of(doc_col, doc_row, rates[h])).astype(bf16)
        state = get_pieces(states, h).astype(bf16)
        inflow = inflow_of(doc_col, doc_row, rates[h])
        whole = dot(grad_weights, key[:, head(h)], 1, 0) + inflow * dot(low, state, 1, 1)
        query_grad[:, head(h)] = whole.astype(bf16)
        key_part[:, head(h)] = dot(grad_weights, query[:, head(h)], 0, 0)
        value_part[:, head(h)] = dot(weights[h], low, 0, 0)


def finish_kernel(rates, docs, key, value, key_part, value_part, states, key_grad, value_grad):
    doc_col, doc_row = docs_of(docs)
    for h in range(LOCAL):
        low = get_pieces(states, h).astype(bf16)
        outflow = outflow_of(doc_col, doc_row, rates[h])
        more = outflow * dot(value[:, head(h)], low, 1, 1)
        key_grad[:, head(h)] = (key_part[:, head(h)] + more).astype(bf16)
        more = outflow * dot(key[:, head(h)], low, 1, 0)
        value_grad[:, head(h)] = (value_part[:, head(h)] + more).astype(bf16)


def place():
    mine = lax.axis_index("seq")
    return mine // (GROUPS * MEMBERS), (mine // MEMBERS) % GROUPS


def my_rate(rates):
    return rates[place()[0] * LOCAL // ROWS]


def faded(rate, blocks):
    return jnp.exp(jnp.full((1, BLOCK), -BLOCK * blocks, f32) * rate)


def passing(same, fade):
    return jnp.where(same, fade, 0.0)


def first_doc(pieces, x, i):
    row = pieces[x * MEMBERS + i, PIECE : PIECE + 1, 0:1]
    return jnp.broadcast_to(row, (1, BLOCK))


def last_doc(pieces, x, i):
    row = pieces[x * MEMBERS + i, PIECE : PIECE + 1, BLOCK - 1 :]
    return jnp.broadcast_to(row, (1, BLOCK))


def state_of(total, x):
    return total[x * PIECE : (x + 1) * PIECE, :]


def doc_of(total, x):
    return total[DOC + x : DOC + x + 1, :]


def group_total_kernel(rates, pieces, out):
    fade = faded(my_rate(rates), 1.0)
    out[DOC:, :] = jnp.zeros((TALL - DOC, BLOCK), f32)
    for x in range(ROWS):
        total = pieces[x * MEMBERS, 0:PIECE, :]
        for i in range(1, MEMBERS):
            same = last_doc(pieces, x, i) == last_doc(pieces, x, i - 1)
            total = passing(same, fade) * total + pieces[x * MEMBERS + i, 0:PIECE, :]
        out[x * PIECE : (x + 1) * PIECE, :] = total
        out[DOC + x : DOC + x + 1, :] = last_doc(pieces, x, MEMBERS - 1)


def pair_total_kernel(rates, mine, theirs, out):
    first = place()[1] % 2 == 0
    fade = faded(my_rate(rates), 1.0 * MEMBERS)
    out[DOC:, :] = jnp.where(first, theirs[DOC:, :], mine[DOC:, :])
    for x in range(ROWS):
        same = doc_of(mine, x) == doc_of(theirs, x)
        low = jnp.where(first, state_of(mine, x), state_of(theirs, x))
        high = jnp.where(first, state_of(theirs, x), state_of(mine, x))
        out[x * PIECE : (x + 1) * PIECE, :] = passing(same, fade) * low + high


def row_docs(mine, theirs, group, x):
    low = jnp.where(group < 2, doc_of(mine, x), doc_of(theirs, x))
    high = jnp.where(group < 2, doc_of(theirs, x), doc_of(mine, x))
    return low, high


def before_group(partner, mine, theirs, group, x):
    low, _ = row_docs(mine, theirs, group, x)
    before = row_docs(mine, theirs, group, x - 1)[1] if x else -jnp.ones((1, BLOCK), f32)
    pair = jnp.where(group > 1, low, before)
    return before, pair, jnp.where(group % 2 == 1, doc_of(partner, x), pair)


def states_kernel(rates, pieces, partner, mine, theirs, out):
    group, rate = place()[1], my_rate(rates)
    one, four = faded(rate, 1.0), faded(rate, 1.0 * MEMBERS)
    eight = faded(rate, 2.0 * MEMBERS)
    carry = jnp.zeros((PIECE, BLOCK), f32)
    for x in range(ROWS):
        before, pair_doc, prev = before_group(partner, mine, theirs, group, x)
        low_doc, high_doc = row_docs(mine, theirs, group, x)
        low = jnp.where(group < 2, state_of(mine, x), state_of(theirs, x))
        high = jnp.where(group < 2, state_of(theirs, x), state_of(mine, x))
        half = passing(low_doc == before, eight) * carry + low
        state = jnp.where(group > 1, half, carry)
        longer = passing(doc_of(partner, x) == pair_doc, four) * state + state_of(partner, x)
        state = jnp.where(group % 2 == 1, longer, state)
        carry = passing(high_doc == low_doc, eight) * half + high
        for i in range(MEMBERS):
            out[x * MEMBERS + i] = passing(first_doc(pieces, x, i) == prev, 1.0) * state
            last = last_doc(pieces, x, i)
            if i < MEMBERS - 1:
                state = passing(last == prev, one) * state + pieces[x * MEMBERS + i, 0:PIECE, :]
            prev = last


def back_total_kernel(rates, pieces, partner, mine, theirs, grads, out):
    group, fade = place()[1], faded(my_rate(rates), 1.0)
    for x in range(ROWS):
        _, _, prev = before_group(partner, mine, theirs, group, x)
        total = jnp.zeros((PIECE, BLOCK), f32)
        for i in range(MEMBERS - 1, -1, -1):
            older = last_doc(pieces, x, i - 1) if i else prev
            local = passing(first_doc(pieces, x, i) == older, 1.0) * grads[x * MEMBERS + i]
            total = passing(last_doc(pieces, x, i) == older, fade) * total + local
        out[x * PIECE : (x + 1) * PIECE, :] = total


def back_pair_kernel(rates, total, partner, mine, theirs, grad, grad_theirs, out):
    group, fade = place()[1], faded(my_rate(rates), 1.0 * MEMBERS)
    first = group % 2 == 0
    for x in range(ROWS):
        _, before, _ = before_group(partner, mine, theirs, group, x)
        low_doc = jnp.where(first, doc_of(total, x), doc_of(partner, x))
        low = jnp.where(first, state_of(grad, x), state_of(grad_theirs, x))
        high = jnp.where(first, state_of(grad_theirs, x), state_of(grad, x))
        out[x * PIECE : (x + 1) * PIECE, :] = low + passing(low_doc == before, fade) * high


def back_states_kernel(
    rates, pieces, total, partner, mine, theirs, grads, partner_grad, pair_grad, other_grad, out
):
    group, rate = place()[1], my_rate(rates)
    one, four = faded(rate, 1.0), faded(rate, 1.0 * MEMBERS)
    eight = faded(rate, 2.0 * MEMBERS)
    carry = jnp.zeros((PIECE, BLOCK), f32)
    for x in range(ROWS - 1, -1, -1):
        before, _, _ = before_group(partner, mine, theirs, group, x)
        low_doc, high_doc = row_docs(mine, theirs, group, x)
        low = jnp.where(group < 2, state_of(pair_grad, x), state_of(other_grad, x))
        high = jnp.where(group < 2, state_of(other_grad, x), state_of(pair_grad, x))
        half = high + passing(high_doc == low_doc, eight) * carry
        state = jnp.where(group < 2, half, carry)
        same = doc_of(total, x) == doc_of(partner, x)
        longer = state_of(partner_grad, x) + passing(same, four) * state
        state = jnp.where(group % 2 == 0, longer, state)
        carry = low + passing(low_doc == before, eight) * half
        for i in range(MEMBERS - 1, -1, -1):
            out[x * MEMBERS + i] = state
            if i:
                last, older = last_doc(pieces, x, i), last_doc(pieces, x, i - 1)
                local = passing(first_doc(pieces, x, i) == older, 1.0) * grads[x * MEMBERS + i]
                state = passing(last == older, one) * state + local


def call(kernel, name, outs, *args, flops=1):
    shapes = [jax.ShapeDtypeStruct(shape, dtype) for shape, dtype in outs]
    moved = sum(a.size * a.dtype.itemsize for a in (*args, *shapes))
    out = pl.pallas_call(
        kernel,
        out_shape=shapes,
        in_specs=[SMEM] + [VMEM] * (len(args) - 1),
        out_specs=[VMEM] * len(shapes),
        name=name,
        compiler_params=pltpu.CompilerParams(vmem_limit_bytes=32 * 1024 * 1024),
        cost_estimate=pl.CostEstimate(flops=flops, bytes_accessed=moved, transcendentals=0),
    )(*args)
    return out[0] if len(out) == 1 else out


def per_device(query, key, value, grad, gain, rates, doc_ids):
    row_len = GROUPS * MEMBERS
    blocks = range(ROWS * row_len)
    owners = [
        [x * row_len + k * MEMBERS + i for x in range(ROWS) for i in range(MEMBERS)] for k in range(GROUPS)
    ]
    swap = functools.partial(
        lax.all_to_all, axis_name="seq", split_axis=0, concat_axis=0, axis_index_groups=owners, tiled=True
    )

    def other_group(total, d):
        return lax.ppermute(total, "seq", [(i, i ^ (d * MEMBERS)) for i in blocks])

    docs = doc_ids.reshape(1, BLOCK)
    gain = gain.reshape(1, LOCAL * HEAD_DIM)
    wide = (BLOCK, LOCAL * HEAD_DIM)
    cut = (OWNERS, PIECE, HEAD_DIM)
    one = 2 * LOCAL * BLOCK * BLOCK * HEAD_DIM

    local = call(
        local_state_kernel, "local_state", [((OWNERS, PIECE + PAD, HEAD_DIM), f32)],
        rates, docs, key, value, flops=one,
    )
    pieces = swap(local)
    total = call(group_total_kernel, "group_total", [((TALL, HEAD_DIM), f32)], rates, pieces)
    partner = other_group(total, 1)
    weights, intra = call(
        intra_kernel, "intra", [((LOCAL, BLOCK, BLOCK), bf16), (wide, f32)],
        rates, docs, query, key, value, flops=2 * one,
    )
    pair = call(pair_total_kernel, "pair_total", [((TALL, HEAD_DIM), f32)], rates, total, partner)
    other = other_group(pair, 3)
    states = swap(call(states_kernel, "states", [(cut, f32)], rates, pieces, partner, pair, other))
    attended, sums = call(
        attend_kernel, "attend", [(wide, f32), ((8, 2, BLOCK), f32)],
        rates, docs, gain, query, grad, intra, states, flops=one,
    )
    sums = lax.all_to_all(sums, "head", 0, 0, tiled=True)
    low_grad, local_grad = call(
        grad_kernel, "grad", [(wide, bf16), (cut, f32)],
        rates, docs, gain, query, grad, attended, sums, flops=one,
    )
    grads = swap(local_grad)
    total_grad = call(
        back_total_kernel, "back_total", [((DOC, HEAD_DIM), f32)], rates, pieces, partner, pair, other, grads
    )
    partner_grad = other_group(total_grad, 1)
    query_grad, key_part, value_part = call(
        back_intra_kernel, "back_intra", [(wide, bf16), (wide, f32), (wide, f32)],
        rates, docs, query, key, value, weights, low_grad, states, flops=5 * one,
    )
    pair_grad = call(
        back_pair_kernel, "back_pair", [((DOC, HEAD_DIM), f32)],
        rates, total, partner, pair, other, total_grad, partner_grad,
    )
    other_grad = other_group(pair_grad, 3)
    states_out = call(
        back_states_kernel, "back_states", [(cut, f32)],
        rates, pieces, total, partner, pair, other, grads, partner_grad, pair_grad, other_grad,
    )
    states_out = swap(states_out)
    key_grad, value_grad = call(
        finish_kernel, "finish", [(wide, bf16), (wide, bf16)],
        rates, docs, key, value, key_part, value_part, states_out, flops=2 * one,
    )
    return query_grad, key_grad, value_grad


def solution(mesh):
    return jax.shard_map(
        per_device,
        mesh=mesh,
        in_specs=(
            P("seq", "head"),
            P("seq", "head"),
            P("seq", "head"),
            P("seq", "head"),
            P("head"),
            P("head"),
            P("seq"),
        ),
        out_specs=(P("seq", "head"), P("seq", "head"), P("seq", "head")),
        check_vma=False,
    )
```

```python
import functools

import jax
import jax.numpy as jnp
from jax import lax
from jax.experimental import pallas as pl
from jax.experimental.pallas import tpu as pltpu
from jax.sharding import PartitionSpec as P

HEADS = 32
HEAD_DIM = 128
BLOCK = 128
LOCAL = 4
MEMBERS = 4
GROUPS = 4
ROWS = 4
OWNERS = ROWS * MEMBERS
PIECE = LOCAL * HEAD_DIM // OWNERS
PAD = 8
DOC = ROWS * PIECE
TALL = DOC + 8

epsilon = 1e-06
f32 = jnp.float32
bf16 = jnp.bfloat16

VMEM = pl.BlockSpec(memory_space=pltpu.VMEM)
SMEM = pl.BlockSpec(memory_space=pltpu.SMEM)


def dot(a, b, a_dim, b_dim):
    return lax.dot_general(a, b, (((a_dim,), (b_dim,)), ((), ())), preferred_element_type=f32)


def square(row):
    return jnp.broadcast_to(row, (BLOCK, BLOCK))


def iota(axis):
    return lax.broadcasted_iota(jnp.int32, (BLOCK, BLOCK), axis).astype(f32)


def head(h):
    return slice(h * HEAD_DIM, (h + 1) * HEAD_DIM)


def outflow_of(doc_col, doc_row, rate):
    last = doc_row[:, BLOCK - 1 :]
    return jnp.where(doc_col == last, jnp.exp(-rate * (BLOCK - 1.0 - iota(0))), 0.0)


def inflow_of(doc_col, doc_row, rate):
    return jnp.where(doc_col == doc_row[:, 0:1], jnp.exp(-rate * (iota(0) + 1.0)), 0.0)


def decays_of(doc_col, doc_row, rate):
    offset = iota(0) - iota(1)
    inside = (offset >= 0.0) & (doc_col == doc_row)
    return jnp.where(inside, jnp.exp(-rate * jnp.maximum(offset, 0.0)), 0.0)


def docs_of(docs):
    row = docs[...].astype(f32)
    return square(row).T, row


def put_pieces(out, h, matrix):
    each = OWNERS // LOCAL
    for i in range(each):
        out[h * each + i, 0:PIECE, :] = matrix[i * PIECE : (i + 1) * PIECE]


def get_pieces(pieces, h):
    each = OWNERS // LOCAL
    return jnp.concatenate([pieces[h * each + i] for i in range(each)], axis=0)


def local_state_kernel(
    rates_in, docs_in, key_in, value_in, out, fades, rates, docs, key, value, sems
):
    pairs = ((rates_in, rates), (docs_in, docs), (key_in, key), (value_in, value))
    copies = [pltpu.make_async_copy(a, b, sems.at[i]) for i, (a, b) in enumerate(pairs)]
    for copy in copies:
        copy.start()
    for copy in copies:
        copy.wait()
    doc_col, doc_row = docs_of(docs)
    for h in range(LOCAL):
        outflow = outflow_of(doc_col, doc_row, rates[h])
        key_out = (key[:, head(h)].astype(f32) * outflow).astype(bf16)
        put_pieces(out, h, dot(key_out, value[:, head(h)], 0, 0))
    for i in range(OWNERS):
        out[i, PIECE:, :] = jnp.broadcast_to(doc_row, (PAD, BLOCK))
    mine = rates[place()[0] * LOCAL // ROWS]
    for i, blocks in enumerate((1, MEMBERS, 2 * MEMBERS)):
        fades[i : i + 1, :] = jnp.exp(jnp.full((1, BLOCK), -1.0 * BLOCK * blocks, f32) * mine)


def intra_kernel(
    rates, docs, gain, query, key, value, grad, weights, attended, scaled, query_in, inflows, outflows
):
    doc_col, doc_row = docs_of(docs)
    scaled[...] = gain[...] * grad[...].astype(f32)
    for h in range(LOCAL):
        scores = dot(query[:, head(h)], key[:, head(h)], 1, 1)
        low = (scores * decays_of(doc_col, doc_row, rates[h])).astype(bf16)
        weights[h] = low
        attended[:, head(h)] = dot(low, value[:, head(h)], 1, 0)
        inflow = inflow_of(doc_col, doc_row, rates[h])
        inflows[h] = inflow
        query_in[:, head(h)] = (query[:, head(h)].astype(f32) * inflow).astype(bf16)
        outflows[h] = outflow_of(doc_col, doc_row, rates[h])


def attend_kernel(inflow, query, scaled, intra, states, attended, sums):
    squares = jnp.zeros((BLOCK, BLOCK), f32)
    crosses = jnp.zeros((BLOCK, BLOCK), f32)
    for h in range(LOCAL):
        low = get_pieces(states, h).astype(bf16)
        whole = intra[:, head(h)] + inflow[h] * dot(query[:, head(h)], low, 1, 0)
        attended[:, head(h)] = whole
        squares = squares + whole * whole
        crosses = crosses + scaled[:, head(h)] * whole
    square_row = jnp.sum(squares.T, axis=0, keepdims=True)
    cross_row = jnp.sum(crosses.T, axis=0, keepdims=True)
    for i in range(sums.shape[0]):
        sums[i, 0:1, :] = square_row
        sums[i, 1:2, :] = cross_row


def grad_kernel(query_in, scaled, attended, sums, low_grad, out):
    both = jnp.sum(sums[...], axis=0)
    width = HEADS * HEAD_DIM
    inv_rms = lax.rsqrt(both[0:1] / width + epsilon)
    slope = both[1:2] * (inv_rms * inv_rms * inv_rms) / width
    inv_col, slope_col = square(inv_rms).T, square(slope).T
    for h in range(LOCAL):
        low = (scaled[:, head(h)] * inv_col - attended[:, head(h)] * slope_col).astype(bf16)
        low_grad[:, head(h)] = low
        put_pieces(out, h, dot(query_in[:, head(h)], low, 0, 0))


def back_intra_kernel(
    rates, docs, inflow, query, key, value, weights, low_grad, states, query_grad, key_part, value_part
):
    doc_col, doc_row = docs_of(docs)
    for h in range(LOCAL):
        low = low_grad[:, head(h)]
        scores = dot(low, value[:, head(h)], 1, 1)
        grad_weights = (scores * decays_of(doc_col, doc_row, rates[h])).astype(bf16)
        state = get_pieces(states, h).astype(bf16)
        whole = dot(grad_weights, key[:, head(h)], 1, 0) + inflow[h] * dot(low, state, 1, 1)
        query_grad[:, head(h)] = whole.astype(bf16)
        key_part[:, head(h)] = dot(grad_weights, query[:, head(h)], 0, 0)
        value_part[:, head(h)] = dot(weights[h], low, 0, 0)


def finish_kernel(outflow, key, value, key_part, value_part, states, key_grad, value_grad):
    for h in range(LOCAL):
        low = get_pieces(states, h).astype(bf16)
        more = outflow[h] * dot(value[:, head(h)], low, 1, 1)
        key_grad[:, head(h)] = (key_part[:, head(h)] + more).astype(bf16)
        more = outflow[h] * dot(key[:, head(h)], low, 1, 0)
        value_grad[:, head(h)] = (value_part[:, head(h)] + more).astype(bf16)


def place():
    mine = lax.axis_index("seq")
    return mine // (GROUPS * MEMBERS), (mine // MEMBERS) % GROUPS


def passing(same, fade):
    return jnp.where(same, fade, 0.0)


def first_doc(pieces, x, i):
    row = pieces[x * MEMBERS + i, PIECE : PIECE + 1, 0:1]
    return jnp.broadcast_to(row, (1, BLOCK))


def last_doc(pieces, x, i):
    row = pieces[x * MEMBERS + i, PIECE : PIECE + 1, BLOCK - 1 :]
    return jnp.broadcast_to(row, (1, BLOCK))


def state_of(total, x):
    return total[x * PIECE : (x + 1) * PIECE, :]


def doc_of(total, x):
    return total[DOC + x : DOC + x + 1, :]


def group_total_kernel(fades, pieces, out):
    fade = fades[0:1, :]
    out[DOC:, :] = jnp.zeros((TALL - DOC, BLOCK), f32)
    for x in range(ROWS):
        total = pieces[x * MEMBERS, 0:PIECE, :]
        for i in range(1, MEMBERS):
            same = last_doc(pieces, x, i) == last_doc(pieces, x, i - 1)
            total = passing(same, fade) * total + pieces[x * MEMBERS + i, 0:PIECE, :]
        out[x * PIECE : (x + 1) * PIECE, :] = total
        out[DOC + x : DOC + x + 1, :] = last_doc(pieces, x, MEMBERS - 1)


def pair_total_kernel(fades, mine, theirs, out):
    first = place()[1] % 2 == 0
    fade = fades[1:2, :]
    out[DOC:, :] = jnp.where(first, theirs[DOC:, :], mine[DOC:, :])
    for x in range(ROWS):
        same = doc_of(mine, x) == doc_of(theirs, x)
        low = jnp.where(first, state_of(mine, x), state_of(theirs, x))
        high = jnp.where(first, state_of(theirs, x), state_of(mine, x))
        out[x * PIECE : (x + 1) * PIECE, :] = passing(same, fade) * low + high


def row_docs(mine, theirs, group, x):
    low = jnp.where(group < 2, doc_of(mine, x), doc_of(theirs, x))
    high = jnp.where(group < 2, doc_of(theirs, x), doc_of(mine, x))
    return low, high


def before_group(partner, mine, theirs, group, x):
    low, _ = row_docs(mine, theirs, group, x)
    before = row_docs(mine, theirs, group, x - 1)[1] if x else -jnp.ones((1, BLOCK), f32)
    pair = jnp.where(group > 1, low, before)
    return before, pair, jnp.where(group % 2 == 1, doc_of(partner, x), pair)


def states_kernel(fades, pieces, partner, mine, theirs, out):
    group = place()[1]
    one, four, eight = fades[0:1, :], fades[1:2, :], fades[2:3, :]
    carry = jnp.zeros((PIECE, BLOCK), f32)
    for x in range(ROWS):
        before, pair_doc, prev = before_group(partner, mine, theirs, group, x)
        low_doc, high_doc = row_docs(mine, theirs, group, x)
        low = jnp.where(group < 2, state_of(mine, x), state_of(theirs, x))
        high = jnp.where(group < 2, state_of(theirs, x), state_of(mine, x))
        half = passing(low_doc == before, eight) * carry + low
        state = jnp.where(group > 1, half, carry)
        longer = passing(doc_of(partner, x) == pair_doc, four) * state + state_of(partner, x)
        state = jnp.where(group % 2 == 1, longer, state)
        carry = passing(high_doc == low_doc, eight) * half + high
        for i in range(MEMBERS):
            out[x * MEMBERS + i] = passing(first_doc(pieces, x, i) == prev, 1.0) * state
            last = last_doc(pieces, x, i)
            if i < MEMBERS - 1:
                state = passing(last == prev, one) * state + pieces[x * MEMBERS + i, 0:PIECE, :]
            prev = last


def back_total_kernel(fades, pieces, partner, mine, theirs, grads, out):
    group, fade = place()[1], fades[0:1, :]
    for x in range(ROWS):
        _, _, prev = before_group(partner, mine, theirs, group, x)
        total = jnp.zeros((PIECE, BLOCK), f32)
        for i in range(MEMBERS - 1, -1, -1):
            older = last_doc(pieces, x, i - 1) if i else prev
            local = passing(first_doc(pieces, x, i) == older, 1.0) * grads[x * MEMBERS + i]
            total = passing(last_doc(pieces, x, i) == older, fade) * total + local
        out[x * PIECE : (x + 1) * PIECE, :] = total


def back_pair_kernel(fades, total, partner, mine, theirs, grad, grad_theirs, out):
    group, fade = place()[1], fades[1:2, :]
    first = group % 2 == 0
    for x in range(ROWS):
        _, before, _ = before_group(partner, mine, theirs, group, x)
        low_doc = jnp.where(first, doc_of(total, x), doc_of(partner, x))
        low = jnp.where(first, state_of(grad, x), state_of(grad_theirs, x))
        high = jnp.where(first, state_of(grad_theirs, x), state_of(grad, x))
        out[x * PIECE : (x + 1) * PIECE, :] = low + passing(low_doc == before, fade) * high


def back_states_kernel(
    fades, pieces, total, partner, mine, theirs, grads, partner_grad, pair_grad, other_grad, out
):
    group = place()[1]
    one, four, eight = fades[0:1, :], fades[1:2, :], fades[2:3, :]
    carry = jnp.zeros((PIECE, BLOCK), f32)
    for x in range(ROWS - 1, -1, -1):
        before, _, _ = before_group(partner, mine, theirs, group, x)
        low_doc, high_doc = row_docs(mine, theirs, group, x)
        low = jnp.where(group < 2, state_of(pair_grad, x), state_of(other_grad, x))
        high = jnp.where(group < 2, state_of(other_grad, x), state_of(pair_grad, x))
        half = high + passing(high_doc == low_doc, eight) * carry
        state = jnp.where(group < 2, half, carry)
        same = doc_of(total, x) == doc_of(partner, x)
        longer = state_of(partner_grad, x) + passing(same, four) * state
        state = jnp.where(group % 2 == 0, longer, state)
        carry = low + passing(low_doc == before, eight) * half
        for i in range(MEMBERS - 1, -1, -1):
            out[x * MEMBERS + i] = state
            if i:
                last, older = last_doc(pieces, x, i), last_doc(pieces, x, i - 1)
                local = passing(first_doc(pieces, x, i) == older, 1.0) * grads[x * MEMBERS + i]
                state = passing(last == older, one) * state + local


def call(kernel, name, outs, *args, flops=1):
    scalars = args[0].shape == (LOCAL,)
    shapes = [jax.ShapeDtypeStruct(shape, dtype) for shape, dtype in outs]
    moved = sum(a.size * a.dtype.itemsize for a in (*args, *shapes))
    out = pl.pallas_call(
        kernel,
        out_shape=shapes,
        in_specs=[SMEM if scalars else VMEM] + [VMEM] * (len(args) - 1),
        out_specs=[VMEM] * len(shapes),
        name=name,
        compiler_params=pltpu.CompilerParams(vmem_limit_bytes=32 * 1024 * 1024),
        cost_estimate=pl.CostEstimate(flops=flops, bytes_accessed=moved, transcendentals=0),
    )(*args)
    return out[0] if len(out) == 1 else out


def per_device(query, key, value, grad, gain, rates, doc_ids):
    row_len = GROUPS * MEMBERS
    blocks = range(ROWS * row_len)
    owners = [
        [x * row_len + k * MEMBERS + i for x in range(ROWS) for i in range(MEMBERS)] for k in range(GROUPS)
    ]
    swap = functools.partial(
        lax.all_to_all, axis_name="seq", split_axis=0, concat_axis=0, axis_index_groups=owners, tiled=True
    )

    def other_group(total, d):
        return lax.ppermute(total, "seq", [(i, i ^ (d * MEMBERS)) for i in blocks])

    docs = doc_ids.reshape(1, BLOCK)
    gain = gain.reshape(1, LOCAL * HEAD_DIM)
    wide = (BLOCK, LOCAL * HEAD_DIM)
    each = (LOCAL, BLOCK, BLOCK)
    cut = (OWNERS, PIECE, HEAD_DIM)
    one = 2 * LOCAL * BLOCK * BLOCK * HEAD_DIM

    local, fades = pl.pallas_call(
        local_state_kernel,
        out_shape=[
            jax.ShapeDtypeStruct((OWNERS, PIECE + PAD, HEAD_DIM), f32),
            jax.ShapeDtypeStruct((8, BLOCK), f32),
        ],
        in_specs=[pl.BlockSpec(memory_space=pl.ANY)] * 4,
        out_specs=[VMEM] * 2,
        scratch_shapes=[
            pltpu.SMEM((LOCAL,), f32),
            pltpu.VMEM((1, BLOCK), jnp.int32),
            pltpu.VMEM(wide, bf16),
            pltpu.VMEM(wide, bf16),
            pltpu.SemaphoreType.DMA((4,)),
        ],
        name="local_state",
        compiler_params=pltpu.CompilerParams(vmem_limit_bytes=60 * 1024 * 1024),
        cost_estimate=pl.CostEstimate(flops=one, bytes_accessed=1 << 19, transcendentals=0),
    )(rates, docs, key, value)
    pieces = swap(local)
    total = call(group_total_kernel, "group_total", [((TALL, HEAD_DIM), f32)], fades, pieces)
    partner = other_group(total, 1)
    weights, intra, scaled, query_in, inflow, outflow = call(
        intra_kernel, "intra",
        [(each, bf16), (wide, f32), (wide, f32), (wide, bf16), (each, f32), (each, f32)],
        rates, docs, gain, query, key, value, grad, flops=2 * one,
    )
    partner, weights, intra = lax.optimization_barrier((partner, weights, intra))
    pair = call(pair_total_kernel, "pair_total", [((TALL, HEAD_DIM), f32)], fades, total, partner)
    other = other_group(pair, 3)
    states = swap(call(states_kernel, "states", [(cut, f32)], fades, pieces, partner, pair, other))
    attended, sums = call(
        attend_kernel, "attend", [(wide, f32), ((8, 2, BLOCK), f32)],
        inflow, query, scaled, intra, states, flops=one,
    )
    sums = lax.all_to_all(sums, "head", 0, 0, tiled=True)
    low_grad, local_grad = call(
        grad_kernel, "grad", [(wide, bf16), (cut, f32)],
        query_in, scaled, attended, sums, flops=one,
    )
    grads = swap(local_grad)
    total_grad = call(
        back_total_kernel, "back_total", [((DOC, HEAD_DIM), f32)], fades, pieces, partner, pair, other, grads
    )
    partner_grad = other_group(total_grad, 1)
    query_grad, key_part, value_part = call(
        back_intra_kernel, "back_intra", [(wide, bf16), (wide, f32), (wide, f32)],
        rates, docs, inflow, query, key, value, weights, low_grad, states, flops=5 * one,
    )
    partner_grad, key_part, value_part = lax.optimization_barrier((partner_grad, key_part, value_part))
    pair_grad = call(
        back_pair_kernel, "back_pair", [((DOC, HEAD_DIM), f32)],
        fades, total, partner, pair, other, total_grad, partner_grad,
    )
    other_grad = other_group(pair_grad, 3)
    states_out = call(
        back_states_kernel, "back_states", [(cut, f32)],
        fades, pieces, total, partner, pair, other, grads, partner_grad, pair_grad, other_grad,
    )
    states_out = swap(states_out)
    key_grad, value_grad = call(
        finish_kernel, "finish", [(wide, bf16), (wide, bf16)],
        outflow, key, value, key_part, value_part, states_out, flops=2 * one,
    )
    return query_grad, key_grad, value_grad


def solution(mesh):
    return jax.shard_map(
        per_device,
        mesh=mesh,
        in_specs=(
            P("seq", "head"),
            P("seq", "head"),
            P("seq", "head"),
            P("seq", "head"),
            P("head"),
            P("head"),
            P("seq"),
        ),
        out_specs=(P("seq", "head"), P("seq", "head"), P("seq", "head")),
        check_vma=False,
    )
```

```python
import functools

import jax
import jax.numpy as jnp
from jax import lax
from jax.experimental import pallas as pl
from jax.experimental.pallas import tpu as pltpu
from jax.sharding import PartitionSpec as P

HEADS = 32
HEAD_DIM = 128
BLOCK = 128
LOCAL = 4
MEMBERS = 4
GROUPS = 4
ROWS = 4
OWNERS = ROWS * MEMBERS
PIECE = LOCAL * HEAD_DIM // OWNERS
SENT = PIECE + 1
DOC = ROWS * PIECE
TALL = DOC + 8

epsilon = 1e-06
f32 = jnp.float32
bf16 = jnp.bfloat16

VMEM = pl.BlockSpec(memory_space=pltpu.VMEM)
SMEM = pl.BlockSpec(memory_space=pltpu.SMEM)


def dot(a, b, a_dim, b_dim):
    return lax.dot_general(a, b, (((a_dim,), (b_dim,)), ((), ())), preferred_element_type=f32)


def square(row):
    return jnp.broadcast_to(row, (BLOCK, BLOCK))


def iota(axis):
    return lax.broadcasted_iota(jnp.int32, (BLOCK, BLOCK), axis).astype(f32)


def head(h):
    return slice(h * HEAD_DIM, (h + 1) * HEAD_DIM)


def outflow_of(doc_col, doc_row, rate):
    last = doc_row[:, BLOCK - 1 :]
    return jnp.where(doc_col == last, jnp.exp(-rate * (BLOCK - 1.0 - iota(0))), 0.0)


def inflow_of(doc_col, doc_row, rate):
    return jnp.where(doc_col == doc_row[:, 0:1], jnp.exp(-rate * (iota(0) + 1.0)), 0.0)


def decays_of(doc_col, doc_row, rate):
    offset = iota(0) - iota(1)
    inside = (offset >= 0.0) & (doc_col == doc_row)
    return jnp.where(inside, jnp.exp(-rate * jnp.maximum(offset, 0.0)), 0.0)


def docs_of(docs):
    row = docs[...].astype(f32)
    return square(row).T, row


def put_pieces(out, h, matrix):
    each = OWNERS // LOCAL
    for i in range(each):
        out[h * each + i] = matrix[i * PIECE : (i + 1) * PIECE]


def get_pieces(pieces, h):
    each = OWNERS // LOCAL
    return jnp.concatenate([pieces[h * each + i] for i in range(each)], axis=0)


def local_state_kernel(
    rates_in, docs_in, key_in, value_in, out, fades, rates, docs, key, value, sems
):
    pairs = ((rates_in, rates), (docs_in, docs), (key_in, key), (value_in, value))
    copies = [pltpu.make_async_copy(a, b, sems.at[i]) for i, (a, b) in enumerate(pairs)]
    for copy in copies:
        copy.start()
    for copy in copies:
        copy.wait()
    doc_col, doc_row = docs_of(docs)
    for h in range(LOCAL):
        outflow = outflow_of(doc_col, doc_row, rates[h])
        key_out = (key[:, head(h)].astype(f32) * outflow).astype(bf16)
        state = dot(key_out, value[:, head(h)], 0, 0)
        for i in range(OWNERS // LOCAL):
            start = (h * OWNERS // LOCAL + i) * SENT
            out[start : start + PIECE, :] = state[i * PIECE : (i + 1) * PIECE]
            out[start + PIECE : start + SENT, :] = doc_row
    mine = rates[lax.axis_index("seq") // (GROUPS * MEMBERS) * LOCAL // ROWS]
    for i, blocks in enumerate((1, MEMBERS, 2 * MEMBERS)):
        fades[i : i + 1, :] = jnp.exp(jnp.full((1, BLOCK), -1.0 * BLOCK * blocks, f32) * mine)


def intra_kernel(
    rates, docs, gain, query, key, value, grad, weights, attended, scaled, query_in, inflows, outflows
):
    doc_col, doc_row = docs_of(docs)
    scaled[...] = gain[...] * grad[...].astype(f32)
    for h in range(LOCAL):
        scores = dot(query[:, head(h)], key[:, head(h)], 1, 1)
        low = (scores * decays_of(doc_col, doc_row, rates[h])).astype(bf16)
        weights[h] = low
        attended[:, head(h)] = dot(low, value[:, head(h)], 1, 0)
        inflow = inflow_of(doc_col, doc_row, rates[h])
        inflows[h] = inflow
        query_in[:, head(h)] = (query[:, head(h)].astype(f32) * inflow).astype(bf16)
        outflows[h] = outflow_of(doc_col, doc_row, rates[h])


def attend_kernel(inflow, query, scaled, intra, states, attended, sums):
    squares = jnp.zeros((BLOCK, BLOCK), f32)
    crosses = jnp.zeros((BLOCK, BLOCK), f32)
    for h in range(LOCAL):
        low = get_pieces(states, h).astype(bf16)
        whole = intra[:, head(h)] + inflow[h] * dot(query[:, head(h)], low, 1, 0)
        attended[:, head(h)] = whole
        squares = squares + whole * whole
        crosses = crosses + scaled[:, head(h)] * whole
    square_row = jnp.sum(squares.T, axis=0, keepdims=True)
    cross_row = jnp.sum(crosses.T, axis=0, keepdims=True)
    for i in range(sums.shape[0]):
        sums[i, 0:1, :] = square_row
        sums[i, 1:2, :] = cross_row


def grad_kernel(query_in, scaled, attended, sums, low_grad, out):
    both = jnp.sum(sums[...], axis=0)
    width = HEADS * HEAD_DIM
    inv_rms = lax.rsqrt(both[0:1] / width + epsilon)
    slope = both[1:2] * (inv_rms * inv_rms * inv_rms) / width
    inv_col, slope_col = square(inv_rms).T, square(slope).T
    for h in range(LOCAL):
        low = (scaled[:, head(h)] * inv_col - attended[:, head(h)] * slope_col).astype(bf16)
        low_grad[:, head(h)] = low
        put_pieces(out, h, dot(query_in[:, head(h)], low, 0, 0))


def back_intra_kernel(
    rates, docs, inflow, query, key, value, weights, low_grad, states, query_grad, key_part, value_part
):
    doc_col, doc_row = docs_of(docs)
    for h in range(LOCAL):
        low = low_grad[:, head(h)]
        scores = dot(low, value[:, head(h)], 1, 1)
        grad_weights = (scores * decays_of(doc_col, doc_row, rates[h])).astype(bf16)
        state = get_pieces(states, h).astype(bf16)
        whole = dot(grad_weights, key[:, head(h)], 1, 0) + inflow[h] * dot(low, state, 1, 1)
        query_grad[:, head(h)] = whole.astype(bf16)
        key_part[:, head(h)] = dot(grad_weights, query[:, head(h)], 0, 0)
        value_part[:, head(h)] = dot(weights[h], low, 0, 0)


def finish_kernel(outflow, key, value, key_part, value_part, states, key_grad, value_grad):
    for h in range(LOCAL):
        low = get_pieces(states, h).astype(bf16)
        more = outflow[h] * dot(value[:, head(h)], low, 1, 1)
        key_grad[:, head(h)] = (key_part[:, head(h)] + more).astype(bf16)
        more = outflow[h] * dot(key[:, head(h)], low, 1, 0)
        value_grad[:, head(h)] = (value_part[:, head(h)] + more).astype(bf16)


def place():
    group, odd = (lax.axis_index("seq") // MEMBERS) % GROUPS, lax.axis_index("head") % 2
    turn = (group + odd) % GROUPS
    return turn, odd == 1, (odd == 1) & (turn == 0), (odd == 1) & (turn == 1)


def passing(same, fade):
    return jnp.where(same, fade, 0.0)


def first_doc(pieces, x, i):
    start = (x * MEMBERS + i) * SENT + PIECE
    row = pieces[start : start + 1, 0:1]
    return jnp.broadcast_to(row, (1, BLOCK))


def last_doc(pieces, x, i):
    start = (x * MEMBERS + i) * SENT + PIECE
    row = pieces[start : start + 1, BLOCK - 1 :]
    return jnp.broadcast_to(row, (1, BLOCK))


def piece_of(pieces, x, i):
    start = (x * MEMBERS + i) * SENT
    return pieces[start : start + PIECE, :]


def state_of(total, x):
    return total[x * PIECE : (x + 1) * PIECE, :]


def doc_of(total, x):
    return total[DOC + x : DOC + x + 1, :]


def pick(read, total, x, late, empty):
    soon = read(total, x) if x < ROWS else empty
    return jnp.where(late, read(total, x - 1) if x else empty, soon)


def state_at(total, x, late):
    return pick(state_of, total, x, late, jnp.zeros((PIECE, BLOCK), f32))


def doc_at(total, x, late):
    return pick(doc_of, total, x, late, -jnp.ones((1, BLOCK), f32))


def ordered(first, mine, theirs):
    return jnp.where(first, mine, theirs), jnp.where(first, theirs, mine)


def group_total_kernel(fades, pieces, out):
    fade = fades[0:1, :]
    out[DOC:, :] = jnp.zeros((TALL - DOC, BLOCK), f32)
    for x in range(ROWS):
        total = piece_of(pieces, x, 0)
        for i in range(1, MEMBERS):
            same = last_doc(pieces, x, i) == last_doc(pieces, x, i - 1)
            total = passing(same, fade) * total + piece_of(pieces, x, i)
        out[x * PIECE : (x + 1) * PIECE, :] = total
        out[DOC + x : DOC + x + 1, :] = last_doc(pieces, x, MEMBERS - 1)


def pair_total_kernel(fades, mine, theirs, out):
    turn, _, late, partner_late = place()
    first, fade = turn % 2 == 0, fades[1:2, :]
    out[DOC:, :] = jnp.zeros((TALL - DOC, BLOCK), f32)
    for x in range(ROWS):
        low_doc, high_doc = ordered(first, doc_at(mine, x, late), doc_at(theirs, x, partner_late))
        low, high = ordered(first, state_at(mine, x, late), state_at(theirs, x, partner_late))
        out[x * PIECE : (x + 1) * PIECE, :] = passing(low_doc == high_doc, fade) * low + high
        out[DOC + x : DOC + x + 1, :] = high_doc


def row_docs(mine, theirs, turn, x):
    return ordered(turn < 2, doc_of(mine, x), doc_of(theirs, x))


def before_row(mine, theirs, turn, x):
    return row_docs(mine, theirs, turn, x - 1)[1] if x else -jnp.ones((1, BLOCK), f32)


def before_pair(mine, theirs, turn, x):
    before = before_row(mine, theirs, turn, x)
    return jnp.where(turn > 1, row_docs(mine, theirs, turn, x)[0], before) if x < ROWS else before


def before_group(partner, mine, theirs, x):
    turn, _, _, partner_late = place()
    before = before_pair(mine, theirs, turn, x)
    return jnp.where(turn % 2 == 1, doc_at(partner, x, partner_late), before) if x < ROWS else before


def states_kernel(fades, pieces, partner, mine, theirs, out):
    turn, _, late, partner_late = place()
    one, four, eight = fades[0:1, :], fades[1:2, :], fades[2:3, :]
    carry = jnp.zeros((PIECE, BLOCK), f32)
    entries = []
    for x in range(ROWS):
        low_doc, high_doc = row_docs(mine, theirs, turn, x)
        low, high = ordered(turn < 2, state_of(mine, x), state_of(theirs, x))
        half = passing(low_doc == before_row(mine, theirs, turn, x), eight) * carry + low
        state = jnp.where(turn > 1, half, carry)
        same = doc_at(partner, x, partner_late) == before_pair(mine, theirs, turn, x)
        longer = passing(same, four) * state + state_at(partner, x, partner_late)
        entries.append(jnp.where(turn % 2 == 1, longer, state))
        carry = passing(high_doc == low_doc, eight) * half + high
    entries.append(carry)
    docs = [before_group(partner, mine, theirs, x) for x in range(ROWS + 1)]
    for x in range(ROWS):
        state = jnp.where(late, entries[x + 1], entries[x])
        prev = jnp.where(late, docs[x + 1], docs[x])
        for i in range(MEMBERS):
            out[x * MEMBERS + i] = passing(first_doc(pieces, x, i) == prev, 1.0) * state
            last = last_doc(pieces, x, i)
            if i < MEMBERS - 1:
                state = passing(last == prev, one) * state + piece_of(pieces, x, i)
            prev = last


def back_total_kernel(fades, pieces, partner, mine, theirs, grads, out):
    late, fade = place()[2], fades[0:1, :]
    docs = [before_group(partner, mine, theirs, x) for x in range(ROWS + 1)]
    for x in range(ROWS):
        prev = jnp.where(late, docs[x + 1], docs[x])
        total = jnp.zeros((PIECE, BLOCK), f32)
        for i in range(MEMBERS - 1, -1, -1):
            older = last_doc(pieces, x, i - 1) if i else prev
            local = passing(first_doc(pieces, x, i) == older, 1.0) * grads[x * MEMBERS + i]
            total = passing(last_doc(pieces, x, i) == older, fade) * total + local
        out[x * PIECE : (x + 1) * PIECE, :] = total


def back_pair_kernel(fades, total, partner, mine, theirs, grad, grad_theirs, out):
    turn, odd, late, partner_late = place()
    first, fade = turn % 2 == 0, fades[1:2, :]
    pairs = []
    for x in range(ROWS + 1):
        low_doc = jnp.where(first, doc_at(total, x, late), doc_at(partner, x, partner_late))
        low, high = ordered(first, state_at(grad, x, late), state_at(grad_theirs, x, partner_late))
        same = low_doc == before_pair(mine, theirs, turn, x)
        pairs.append(low + passing(same, fade) * high)
    for x in range(ROWS):
        out[x * PIECE : (x + 1) * PIECE, :] = jnp.where(odd & (turn < 2), pairs[x + 1], pairs[x])


def back_states_kernel(
    fades, pieces, total, partner, mine, theirs, grads, partner_grad, pair_grad, other_grad, out
):
    turn, odd, late, partner_late = place()
    one, four, eight = fades[0:1, :], fades[1:2, :], fades[2:3, :]

    def low_grad(x):
        return jnp.where(turn < 2, state_at(pair_grad, x, odd), state_at(other_grad, x, odd))

    carry = low_grad(ROWS)
    entries = [jnp.zeros((PIECE, BLOCK), f32)]
    for x in range(ROWS - 1, -1, -1):
        low_doc, high_doc = row_docs(mine, theirs, turn, x)
        high = jnp.where(turn < 2, state_of(other_grad, x), state_of(pair_grad, x))
        half = high + passing(high_doc == low_doc, eight) * carry
        state = jnp.where(turn < 2, half, carry)
        same = doc_at(total, x, late) == doc_at(partner, x, partner_late)
        longer = state_at(partner_grad, x, partner_late) + passing(same, four) * state
        entries.insert(0, jnp.where(turn % 2 == 0, longer, state))
        carry = low_grad(x) + passing(low_doc == before_row(mine, theirs, turn, x), eight) * half
    for x in range(ROWS):
        state = jnp.where(late, entries[x + 1], entries[x])
        for i in range(MEMBERS - 1, -1, -1):
            out[x * MEMBERS + i] = state
            if i:
                last, older = last_doc(pieces, x, i), last_doc(pieces, x, i - 1)
                local = passing(first_doc(pieces, x, i) == older, 1.0) * grads[x * MEMBERS + i]
                state = passing(last == older, one) * state + local


def call(kernel, name, outs, *args, flops=1):
    scalars = args[0].shape == (LOCAL,)
    shapes = [jax.ShapeDtypeStruct(shape, dtype) for shape, dtype in outs]
    moved = sum(a.size * a.dtype.itemsize for a in (*args, *shapes))
    out = pl.pallas_call(
        kernel,
        out_shape=shapes,
        in_specs=[SMEM if scalars else VMEM] + [VMEM] * (len(args) - 1),
        out_specs=[VMEM] * len(shapes),
        name=name,
        compiler_params=pltpu.CompilerParams(vmem_limit_bytes=32 * 1024 * 1024),
        cost_estimate=pl.CostEstimate(flops=flops, bytes_accessed=moved, transcendentals=0),
    )(*args)
    return out[0] if len(out) == 1 else out


def per_device(query, key, value, grad, gain, rates, doc_ids):
    row_len = GROUPS * MEMBERS
    blocks = range(ROWS * row_len)
    owners = [
        [x * row_len + k * MEMBERS + i for x in range(ROWS) for i in range(MEMBERS)] for k in range(GROUPS)
    ]
    swap = functools.partial(
        lax.all_to_all, axis_name="seq", split_axis=0, concat_axis=0, axis_index_groups=owners, tiled=True
    )

    heads = lax.axis_size("head")

    def other_group(total, step):
        pairs = [
            (i * heads + h, (i ^ ((1, 3)[(step + h) % 2] * MEMBERS)) * heads + h)
            for i in blocks
            for h in range(heads)
        ]
        return lax.ppermute(total, ("seq", "head"), pairs)

    docs = doc_ids.reshape(1, BLOCK)
    gain = gain.reshape(1, LOCAL * HEAD_DIM)
    wide = (BLOCK, LOCAL * HEAD_DIM)
    each = (LOCAL, BLOCK, BLOCK)
    cut = (OWNERS, PIECE, HEAD_DIM)
    one = 2 * LOCAL * BLOCK * BLOCK * HEAD_DIM

    local, fades = pl.pallas_call(
        local_state_kernel,
        out_shape=[
            jax.ShapeDtypeStruct((OWNERS * SENT, HEAD_DIM), f32),
            jax.ShapeDtypeStruct((8, BLOCK), f32),
        ],
        in_specs=[pl.BlockSpec(memory_space=pl.ANY)] * 4,
        out_specs=[VMEM] * 2,
        scratch_shapes=[
            pltpu.SMEM((LOCAL,), f32),
            pltpu.VMEM((1, BLOCK), jnp.int32),
            pltpu.VMEM(wide, bf16),
            pltpu.VMEM(wide, bf16),
            pltpu.SemaphoreType.DMA((4,)),
        ],
        name="local_state",
        compiler_params=pltpu.CompilerParams(vmem_limit_bytes=60 * 1024 * 1024),
        cost_estimate=pl.CostEstimate(flops=one, bytes_accessed=1 << 19, transcendentals=0),
    )(rates, docs, key, value)
    pieces = swap(local.reshape(OWNERS, SENT, 1, HEAD_DIM)).reshape(local.shape)
    total = call(group_total_kernel, "group_total", [((TALL, HEAD_DIM), f32)], fades, pieces)
    partner = other_group(total, 0)
    weights, intra, scaled, query_in, inflow, outflow = call(
        intra_kernel, "intra",
        [(each, bf16), (wide, f32), (wide, f32), (wide, bf16), (each, f32), (each, f32)],
        rates, docs, gain, query, key, value, grad, flops=2 * one,
    )
    partner, weights, intra = lax.optimization_barrier((partner, weights, intra))
    pair = call(pair_total_kernel, "pair_total", [((TALL, HEAD_DIM), f32)], fades, total, partner)
    other = other_group(pair, 1)
    states = swap(call(states_kernel, "states", [(cut, f32)], fades, pieces, partner, pair, other))
    attended, sums = call(
        attend_kernel, "attend", [(wide, f32), ((8, 2, BLOCK), f32)],
        inflow, query, scaled, intra, states, flops=one,
    )
    sums = lax.all_to_all(sums, "head", 0, 0, tiled=True)
    low_grad, local_grad = call(
        grad_kernel, "grad", [(wide, bf16), (cut, f32)],
        query_in, scaled, attended, sums, flops=one,
    )
    grads = swap(local_grad)
    total_grad = call(
        back_total_kernel, "back_total", [((DOC, HEAD_DIM), f32)], fades, pieces, partner, pair, other, grads
    )
    partner_grad = other_group(total_grad, 0)
    query_grad, key_part, value_part = call(
        back_intra_kernel, "back_intra", [(wide, bf16), (wide, f32), (wide, f32)],
        rates, docs, inflow, query, key, value, weights, low_grad, states, flops=5 * one,
    )
    partner_grad, key_part, value_part = lax.optimization_barrier((partner_grad, key_part, value_part))
    pair_grad = call(
        back_pair_kernel, "back_pair", [((DOC, HEAD_DIM), f32)],
        fades, total, partner, pair, other, total_grad, partner_grad,
    )
    other_grad = other_group(pair_grad, 1)
    states_out = call(
        back_states_kernel, "back_states", [(cut, f32)],
        fades, pieces, total, partner, pair, other, grads, partner_grad, pair_grad, other_grad,
    )
    states_out = swap(states_out)
    key_grad, value_grad = call(
        finish_kernel, "finish", [(wide, bf16), (wide, bf16)],
        outflow, key, value, key_part, value_part, states_out, flops=2 * one,
    )
    return query_grad, key_grad, value_grad


def solution(mesh):
    return jax.shard_map(
        per_device,
        mesh=mesh,
        in_specs=(
            P("seq", "head"),
            P("seq", "head"),
            P("seq", "head"),
            P("seq", "head"),
            P("head"),
            P("head"),
            P("seq"),
        ),
        out_specs=(P("seq", "head"), P("seq", "head"), P("seq", "head")),
        check_vma=False,
    )
```

```python
import functools

import jax
import jax.numpy as jnp
from jax import lax
from jax.experimental import pallas as pl
from jax.experimental.pallas import tpu as pltpu
from jax.sharding import PartitionSpec as P

HEADS = 32
HEAD_DIM = 128
BLOCK = 128
LOCAL = 4
MEMBERS = 4
GROUPS = 4
ROWS = 4
OWNERS = ROWS * MEMBERS
FLIP = 5
PIECE = LOCAL * HEAD_DIM // OWNERS
SENT = PIECE + 1
DOC = ROWS * PIECE
TALL = DOC + 8

epsilon = 1e-06
f32 = jnp.float32
bf16 = jnp.bfloat16

VMEM = pl.BlockSpec(memory_space=pltpu.VMEM)
SMEM = pl.BlockSpec(memory_space=pltpu.SMEM)


def dot(a, b, a_dim, b_dim):
    return lax.dot_general(a, b, (((a_dim,), (b_dim,)), ((), ())), preferred_element_type=f32)


def square(row):
    return jnp.broadcast_to(row, (BLOCK, BLOCK))


def iota(axis):
    return lax.broadcasted_iota(jnp.int32, (BLOCK, BLOCK), axis).astype(f32)


def head(h):
    return slice(h * HEAD_DIM, (h + 1) * HEAD_DIM)


def outflow_of(doc_col, doc_row, rate):
    last = doc_row[:, BLOCK - 1 :]
    return jnp.where(doc_col == last, jnp.exp(-rate * (BLOCK - 1.0 - iota(0))), 0.0)


def inflow_of(doc_col, doc_row, rate):
    return jnp.where(doc_col == doc_row[:, 0:1], jnp.exp(-rate * (iota(0) + 1.0)), 0.0)


def decays_of(doc_col, doc_row, rate):
    offset = iota(0) - iota(1)
    inside = (offset >= 0.0) & (doc_col == doc_row)
    return jnp.where(inside, jnp.exp(-rate * jnp.maximum(offset, 0.0)), 0.0)


def docs_of(docs):
    row = docs[...].astype(f32)
    return square(row).T, row


def put_pieces(out, h, matrix):
    each = OWNERS // LOCAL
    for i in range(each):
        out[h * each + i] = matrix[i * PIECE : (i + 1) * PIECE]


def get_pieces(pieces, h):
    each = OWNERS // LOCAL
    return jnp.concatenate([pieces[h * each + i] for i in range(each)], axis=0)


def local_state_kernel(
    rates_in, docs_in, key_in, value_in, out, fades, rates, docs, key, value, sems
):
    pairs = ((rates_in, rates), (docs_in, docs), (key_in, key), (value_in, value))
    copies = [pltpu.make_async_copy(a, b, sems.at[i]) for i, (a, b) in enumerate(pairs)]
    for copy in copies:
        copy.start()
    for copy in copies[:2]:
        copy.wait()
    doc_col, doc_row = docs_of(docs)
    outflows = [outflow_of(doc_col, doc_row, rates[h]) for h in range(LOCAL)]
    mine = rates[position(lax.axis_index("seq") // (GROUPS * MEMBERS) * MEMBERS) // MEMBERS * LOCAL // ROWS]
    for i, blocks in enumerate((1, MEMBERS, 2 * MEMBERS)):
        fades[i : i + 1, :] = jnp.exp(jnp.full((1, BLOCK), -1.0 * BLOCK * blocks, f32) * mine)
    for copy in copies[2:]:
        copy.wait()
    for h in range(LOCAL):
        key_out = (key[:, head(h)].astype(f32) * outflows[h]).astype(bf16)
        state = dot(key_out, value[:, head(h)], 0, 0)
        for i in range(OWNERS // LOCAL):
            start = (h * OWNERS // LOCAL + i) * SENT
            out[start : start + PIECE, :] = state[i * PIECE : (i + 1) * PIECE]
            out[start + PIECE : start + SENT, :] = doc_row


def intra_kernel(
    rates, docs, gain, query, key, value, grad, weights, attended, scaled, query_in, inflows, outflows
):
    doc_col, doc_row = docs_of(docs)
    scaled[...] = gain[...] * grad[...].astype(f32)
    for h in range(LOCAL):
        scores = dot(query[:, head(h)], key[:, head(h)], 1, 1)
        low = (scores * decays_of(doc_col, doc_row, rates[h])).astype(bf16)
        weights[h] = low
        attended[:, head(h)] = dot(low, value[:, head(h)], 1, 0)
        inflow = inflow_of(doc_col, doc_row, rates[h])
        inflows[h] = inflow
        query_in[:, head(h)] = (query[:, head(h)].astype(f32) * inflow).astype(bf16)
        outflows[h] = outflow_of(doc_col, doc_row, rates[h])


def attend_kernel(inflow, query, scaled, intra, states, attended, sums):
    squares = jnp.zeros((BLOCK, BLOCK), f32)
    crosses = jnp.zeros((BLOCK, BLOCK), f32)
    for h in range(LOCAL):
        low = get_pieces(states, h).astype(bf16)
        whole = intra[:, head(h)] + inflow[h] * dot(query[:, head(h)], low, 1, 0)
        attended[:, head(h)] = whole
        squares = squares + whole * whole
        crosses = crosses + scaled[:, head(h)] * whole
    square_row = jnp.sum(squares.T, axis=0, keepdims=True)
    cross_row = jnp.sum(crosses.T, axis=0, keepdims=True)
    for i in range(sums.shape[0]):
        sums[i, 0:1, :] = square_row
        sums[i, 1:2, :] = cross_row


def grad_kernel(query_in, scaled, attended, sums, low_grad, out):
    both = jnp.sum(sums[...], axis=0)
    width = HEADS * HEAD_DIM
    inv_rms = lax.rsqrt(both[0:1] / width + epsilon)
    slope = both[1:2] * (inv_rms * inv_rms * inv_rms) / width
    inv_col, slope_col = square(inv_rms).T, square(slope).T
    for h in range(LOCAL):
        low = (scaled[:, head(h)] * inv_col - attended[:, head(h)] * slope_col).astype(bf16)
        low_grad[:, head(h)] = low
        put_pieces(out, h, dot(query_in[:, head(h)], low, 0, 0))


def back_intra_kernel(
    rates, docs, inflow, query, key, value, weights, low_grad, states, query_grad, key_part, value_part
):
    doc_col, doc_row = docs_of(docs)
    for h in range(LOCAL):
        low = low_grad[:, head(h)]
        scores = dot(low, value[:, head(h)], 1, 1)
        grad_weights = (scores * decays_of(doc_col, doc_row, rates[h])).astype(bf16)
        state = get_pieces(states, h).astype(bf16)
        whole = dot(grad_weights, key[:, head(h)], 1, 0) + inflow[h] * dot(low, state, 1, 1)
        query_grad[:, head(h)] = whole.astype(bf16)
        key_part[:, head(h)] = dot(grad_weights, query[:, head(h)], 0, 0)
        value_part[:, head(h)] = dot(weights[h], low, 0, 0)


def finish_kernel(outflow, key, value, key_part, value_part, states, key_grad, value_grad):
    for h in range(LOCAL):
        low = get_pieces(states, h).astype(bf16)
        more = outflow[h] * dot(value[:, head(h)], low, 1, 1)
        key_grad[:, head(h)] = (key_part[:, head(h)] + more).astype(bf16)
        more = outflow[h] * dot(key[:, head(h)], low, 1, 0)
        value_grad[:, head(h)] = (value_part[:, head(h)] + more).astype(bf16)


def place():
    group, odd = (lax.axis_index("seq") // MEMBERS) % GROUPS, (lax.axis_index("head") + 1) % 2
    turn = (group + odd) % GROUPS
    return turn, odd == 1, (odd == 1) & (turn == 0), (odd == 1) & (turn == 1)


def passing(same, fade):
    return jnp.where(same, fade, 0.0)


def flipped():
    return lax.axis_index("head") % 2 == 1


def position(block):
    return jnp.where(flipped(), block ^ FLIP, block)


def slot(x, i):
    return position(x * MEMBERS + i)


def rows_of(pieces, x, i, first, count):
    start = (x * MEMBERS + i) * SENT + first
    other = ((x * MEMBERS + i) ^ FLIP) * SENT + first
    return jnp.where(flipped(), pieces[other : other + count, :], pieces[start : start + count, :])


def first_doc(pieces, x, i):
    return jnp.broadcast_to(rows_of(pieces, x, i, PIECE, 1)[:, 0:1], (1, BLOCK))


def last_doc(pieces, x, i):
    return jnp.broadcast_to(rows_of(pieces, x, i, PIECE, 1)[:, BLOCK - 1 :], (1, BLOCK))


def piece_of(pieces, x, i):
    return rows_of(pieces, x, i, 0, PIECE)


def state_of(total, x):
    return total[x * PIECE : (x + 1) * PIECE, :]


def doc_of(total, x):
    return total[DOC + x : DOC + x + 1, :]


def pick(read, total, x, late, empty):
    soon = read(total, x) if x < ROWS else empty
    return jnp.where(late, read(total, x - 1) if x else empty, soon)


def state_at(total, x, late):
    return pick(state_of, total, x, late, jnp.zeros((PIECE, BLOCK), f32))


def doc_at(total, x, late):
    return pick(doc_of, total, x, late, -jnp.ones((1, BLOCK), f32))


def ordered(first, mine, theirs):
    return jnp.where(first, mine, theirs), jnp.where(first, theirs, mine)


def group_total_kernel(fades, pieces, out):
    fade = fades[0:1, :]
    out[DOC:, :] = jnp.zeros((TALL - DOC, BLOCK), f32)
    for x in range(ROWS):
        total = piece_of(pieces, x, 0)
        for i in range(1, MEMBERS):
            same = last_doc(pieces, x, i) == last_doc(pieces, x, i - 1)
            total = passing(same, fade) * total + piece_of(pieces, x, i)
        out[x * PIECE : (x + 1) * PIECE, :] = total
        out[DOC + x : DOC + x + 1, :] = last_doc(pieces, x, MEMBERS - 1)


def pair_total_kernel(fades, mine, theirs, out):
    turn, _, late, partner_late = place()
    first, fade = turn % 2 == 0, fades[1:2, :]
    out[DOC:, :] = jnp.zeros((TALL - DOC, BLOCK), f32)
    for x in range(ROWS):
        low_doc, high_doc = ordered(first, doc_at(mine, x, late), doc_at(theirs, x, partner_late))
        low, high = ordered(first, state_at(mine, x, late), state_at(theirs, x, partner_late))
        out[x * PIECE : (x + 1) * PIECE, :] = passing(low_doc == high_doc, fade) * low + high
        out[DOC + x : DOC + x + 1, :] = high_doc


def row_docs(mine, theirs, turn, x):
    return ordered(turn < 2, doc_of(mine, x), doc_of(theirs, x))


def before_row(mine, theirs, turn, x):
    return row_docs(mine, theirs, turn, x - 1)[1] if x else -jnp.ones((1, BLOCK), f32)


def before_pair(mine, theirs, turn, x):
    before = before_row(mine, theirs, turn, x)
    return jnp.where(turn > 1, row_docs(mine, theirs, turn, x)[0], before) if x < ROWS else before


def before_group(partner, mine, theirs, x):
    turn, _, _, partner_late = place()
    before = before_pair(mine, theirs, turn, x)
    return jnp.where(turn % 2 == 1, doc_at(partner, x, partner_late), before) if x < ROWS else before


def states_kernel(fades, pieces, partner, mine, theirs, out):
    turn, _, late, partner_late = place()
    one, four, eight = fades[0:1, :], fades[1:2, :], fades[2:3, :]
    carry = jnp.zeros((PIECE, BLOCK), f32)
    entries = []
    for x in range(ROWS):
        low_doc, high_doc = row_docs(mine, theirs, turn, x)
        low, high = ordered(turn < 2, state_of(mine, x), state_of(theirs, x))
        half = passing(low_doc == before_row(mine, theirs, turn, x), eight) * carry + low
        state = jnp.where(turn > 1, half, carry)
        same = doc_at(partner, x, partner_late) == before_pair(mine, theirs, turn, x)
        longer = passing(same, four) * state + state_at(partner, x, partner_late)
        entries.append(jnp.where(turn % 2 == 1, longer, state))
        carry = passing(high_doc == low_doc, eight) * half + high
    entries.append(carry)
    docs = [before_group(partner, mine, theirs, x) for x in range(ROWS + 1)]
    for x in range(ROWS):
        state = jnp.where(late, entries[x + 1], entries[x])
        prev = jnp.where(late, docs[x + 1], docs[x])
        for i in range(MEMBERS):
            out[slot(x, i)] = passing(first_doc(pieces, x, i) == prev, 1.0) * state
            last = last_doc(pieces, x, i)
            if i < MEMBERS - 1:
                state = passing(last == prev, one) * state + piece_of(pieces, x, i)
            prev = last


def back_total_kernel(fades, pieces, partner, mine, theirs, grads, out):
    late, fade = place()[2], fades[0:1, :]
    docs = [before_group(partner, mine, theirs, x) for x in range(ROWS + 1)]
    for x in range(ROWS):
        prev = jnp.where(late, docs[x + 1], docs[x])
        total = jnp.zeros((PIECE, BLOCK), f32)
        for i in range(MEMBERS - 1, -1, -1):
            older = last_doc(pieces, x, i - 1) if i else prev
            local = passing(first_doc(pieces, x, i) == older, 1.0) * grads[slot(x, i)]
            total = passing(last_doc(pieces, x, i) == older, fade) * total + local
        out[x * PIECE : (x + 1) * PIECE, :] = total


def back_pair_kernel(fades, total, partner, mine, theirs, grad, grad_theirs, out):
    turn, odd, late, partner_late = place()
    first, fade = turn % 2 == 0, fades[1:2, :]
    pairs = []
    for x in range(ROWS + 1):
        low_doc = jnp.where(first, doc_at(total, x, late), doc_at(partner, x, partner_late))
        low, high = ordered(first, state_at(grad, x, late), state_at(grad_theirs, x, partner_late))
        same = low_doc == before_pair(mine, theirs, turn, x)
        pairs.append(low + passing(same, fade) * high)
    for x in range(ROWS):
        out[x * PIECE : (x + 1) * PIECE, :] = jnp.where(odd & (turn < 2), pairs[x + 1], pairs[x])


def back_states_kernel(
    fades, pieces, total, partner, mine, theirs, grads, partner_grad, pair_grad, other_grad, out
):
    turn, odd, late, partner_late = place()
    one, four, eight = fades[0:1, :], fades[1:2, :], fades[2:3, :]

    def low_grad(x):
        return jnp.where(turn < 2, state_at(pair_grad, x, odd), state_at(other_grad, x, odd))

    carry = low_grad(ROWS)
    entries = [jnp.zeros((PIECE, BLOCK), f32)]
    for x in range(ROWS - 1, -1, -1):
        low_doc, high_doc = row_docs(mine, theirs, turn, x)
        high = jnp.where(turn < 2, state_of(other_grad, x), state_of(pair_grad, x))
        half = high + passing(high_doc == low_doc, eight) * carry
        state = jnp.where(turn < 2, half, carry)
        same = doc_at(total, x, late) == doc_at(partner, x, partner_late)
        longer = state_at(partner_grad, x, partner_late) + passing(same, four) * state
        entries.insert(0, jnp.where(turn % 2 == 0, longer, state))
        carry = low_grad(x) + passing(low_doc == before_row(mine, theirs, turn, x), eight) * half
    for x in range(ROWS):
        state = jnp.where(late, entries[x + 1], entries[x])
        for i in range(MEMBERS - 1, -1, -1):
            out[slot(x, i)] = state
            if i:
                last, older = last_doc(pieces, x, i), last_doc(pieces, x, i - 1)
                local = passing(first_doc(pieces, x, i) == older, 1.0) * grads[slot(x, i)]
                state = passing(last == older, one) * state + local


def call(kernel, name, outs, *args, flops=1):
    scalars = args[0].shape == (LOCAL,)
    shapes = [jax.ShapeDtypeStruct(shape, dtype) for shape, dtype in outs]
    moved = sum(a.size * a.dtype.itemsize for a in (*args, *shapes))
    out = pl.pallas_call(
        kernel,
        out_shape=shapes,
        in_specs=[SMEM if scalars else VMEM] + [VMEM] * (len(args) - 1),
        out_specs=[VMEM] * len(shapes),
        name=name,
        compiler_params=pltpu.CompilerParams(vmem_limit_bytes=32 * 1024 * 1024),
        cost_estimate=pl.CostEstimate(flops=flops, bytes_accessed=moved, transcendentals=0),
    )(*args)
    return out[0] if len(out) == 1 else out


def per_device(query, key, value, grad, gain, rates, doc_ids):
    row_len = GROUPS * MEMBERS
    blocks = range(ROWS * row_len)
    owners = [
        [x * row_len + k * MEMBERS + i for x in range(ROWS) for i in range(MEMBERS)] for k in range(GROUPS)
    ]
    heads = lax.axis_size("head")
    orders = [
        [group[j ^ (FLIP * (h % 2))] * heads + h for j in range(OWNERS)] for group in owners for h in range(heads)
    ]
    swap = functools.partial(
        lax.all_to_all, axis_name=("seq", "head"), split_axis=0, concat_axis=0, axis_index_groups=orders, tiled=True
    )

    def other_group(total, step):
        pairs = [
            (i * heads + h, (i ^ ((1, 3)[(step + h + 1) % 2] * MEMBERS)) * heads + h)
            for i in blocks
            for h in range(heads)
        ]
        return lax.ppermute(total, ("seq", "head"), pairs)

    docs = doc_ids.reshape(1, BLOCK)
    gain = gain.reshape(1, LOCAL * HEAD_DIM)
    wide = (BLOCK, LOCAL * HEAD_DIM)
    each = (LOCAL, BLOCK, BLOCK)
    cut = (OWNERS, PIECE, HEAD_DIM)
    one = 2 * LOCAL * BLOCK * BLOCK * HEAD_DIM

    local, fades = pl.pallas_call(
        local_state_kernel,
        out_shape=[
            jax.ShapeDtypeStruct((OWNERS * SENT, HEAD_DIM), f32),
            jax.ShapeDtypeStruct((8, BLOCK), f32),
        ],
        in_specs=[pl.BlockSpec(memory_space=pl.ANY)] * 4,
        out_specs=[VMEM] * 2,
        scratch_shapes=[
            pltpu.SMEM((LOCAL,), f32),
            pltpu.VMEM((1, BLOCK), jnp.int32),
            pltpu.VMEM(wide, bf16),
            pltpu.VMEM(wide, bf16),
            pltpu.SemaphoreType.DMA((4,)),
        ],
        name="local_state",
        compiler_params=pltpu.CompilerParams(vmem_limit_bytes=60 * 1024 * 1024),
        cost_estimate=pl.CostEstimate(flops=one, bytes_accessed=1 << 19, transcendentals=0),
    )(rates, docs, key, value)
    pieces = swap(local.reshape(OWNERS, SENT, 1, HEAD_DIM)).reshape(local.shape)
    total = call(group_total_kernel, "group_total", [((TALL, HEAD_DIM), f32)], fades, pieces)
    partner = other_group(total, 0)
    weights, intra, scaled, query_in, inflow, outflow = call(
        intra_kernel, "intra",
        [(each, bf16), (wide, f32), (wide, f32), (wide, bf16), (each, f32), (each, f32)],
        rates, docs, gain, query, key, value, grad, flops=2 * one,
    )
    partner, weights, intra = lax.optimization_barrier((partner, weights, intra))
    pair = call(pair_total_kernel, "pair_total", [((TALL, HEAD_DIM), f32)], fades, total, partner)
    other = other_group(pair, 1)
    states = swap(call(states_kernel, "states", [(cut, f32)], fades, pieces, partner, pair, other))
    attended, sums = call(
        attend_kernel, "attend", [(wide, f32), ((8, 2, BLOCK), f32)],
        inflow, query, scaled, intra, states, flops=one,
    )
    sums = lax.all_to_all(sums, "head", 0, 0, tiled=True)
    low_grad, local_grad = call(
        grad_kernel, "grad", [(wide, bf16), (cut, f32)],
        query_in, scaled, attended, sums, flops=one,
    )
    grads = swap(local_grad)
    total_grad = call(
        back_total_kernel, "back_total", [((DOC, HEAD_DIM), f32)], fades, pieces, partner, pair, other, grads
    )
    partner_grad = other_group(total_grad, 0)
    query_grad, key_part, value_part = call(
        back_intra_kernel, "back_intra", [(wide, bf16), (wide, f32), (wide, f32)],
        rates, docs, inflow, query, key, value, weights, low_grad, states, flops=5 * one,
    )
    partner_grad, key_part, value_part = lax.optimization_barrier((partner_grad, key_part, value_part))
    pair_grad = call(
        back_pair_kernel, "back_pair", [((DOC, HEAD_DIM), f32)],
        fades, total, partner, pair, other, total_grad, partner_grad,
    )
    other_grad = other_group(pair_grad, 1)
    states_out = call(
        back_states_kernel, "back_states", [(cut, f32)],
        fades, pieces, total, partner, pair, other, grads, partner_grad, pair_grad, other_grad,
    )
    states_out = swap(states_out)
    key_grad, value_grad = call(
        finish_kernel, "finish", [(wide, bf16), (wide, bf16)],
        outflow, key, value, key_part, value_part, states_out, flops=2 * one,
    )
    return query_grad, key_grad, value_grad


def solution(mesh):
    return jax.shard_map(
        per_device,
        mesh=mesh,
        in_specs=(
            P("seq", "head"),
            P("seq", "head"),
            P("seq", "head"),
            P("seq", "head"),
            P("head"),
            P("head"),
            P("seq"),
        ),
        out_specs=(P("seq", "head"), P("seq", "head"), P("seq", "head")),
        check_vma=False,
    )
```

```python
import functools

import jax
import jax.numpy as jnp
from jax import lax
from jax.experimental import pallas as pl
from jax.experimental.pallas import tpu as pltpu
from jax.sharding import PartitionSpec as P

HEADS = 32
HEAD_DIM = 128
BLOCK = 128
LOCAL = 4
MEMBERS = 4
GROUPS = 4
ROWS = 4
OWNERS = ROWS * MEMBERS
FLIPS = (10, 15)
PIECE = LOCAL * HEAD_DIM // OWNERS
SENT = PIECE + 1
DOC = ROWS * PIECE
TALL = DOC + 8

epsilon = 1e-06
f32 = jnp.float32
bf16 = jnp.bfloat16

VMEM = pl.BlockSpec(memory_space=pltpu.VMEM)
SMEM = pl.BlockSpec(memory_space=pltpu.SMEM)


def dot(a, b, a_dim, b_dim):
    return lax.dot_general(a, b, (((a_dim,), (b_dim,)), ((), ())), preferred_element_type=f32)


def square(row):
    return jnp.broadcast_to(row, (BLOCK, BLOCK))


def iota(axis):
    return lax.broadcasted_iota(jnp.int32, (BLOCK, BLOCK), axis).astype(f32)


def head(h):
    return slice(h * HEAD_DIM, (h + 1) * HEAD_DIM)


def outflow_of(doc_col, doc_row, rate):
    last = doc_row[:, BLOCK - 1 :]
    return jnp.where(doc_col == last, jnp.exp(-rate * (BLOCK - 1.0 - iota(0))), 0.0)


def inflow_of(doc_col, doc_row, rate):
    return jnp.where(doc_col == doc_row[:, 0:1], jnp.exp(-rate * (iota(0) + 1.0)), 0.0)


def decays_of(doc_col, doc_row, rate):
    offset = iota(0) - iota(1)
    inside = (offset >= 0.0) & (doc_col == doc_row)
    return jnp.where(inside, jnp.exp(-rate * jnp.maximum(offset, 0.0)), 0.0)


def docs_of(docs):
    row = docs[...].astype(f32)
    return square(row).T, row


def put_pieces(out, h, matrix):
    each = OWNERS // LOCAL
    for i in range(each):
        out[h * each + i] = matrix[i * PIECE : (i + 1) * PIECE]


def get_pieces(pieces, h):
    each = OWNERS // LOCAL
    return jnp.concatenate([pieces[h * each + i] for i in range(each)], axis=0)


def local_state_kernel(
    rates_in, docs_in, key_in, value_in, out, fades, rates, docs, key, value, sems
):
    pairs = ((rates_in, rates), (docs_in, docs), (key_in, key), (value_in, value))
    copies = [pltpu.make_async_copy(a, b, sems.at[i]) for i, (a, b) in enumerate(pairs)]
    for copy in copies:
        copy.start()
    for copy in copies[:2]:
        copy.wait()
    doc_col, doc_row = docs_of(docs)
    outflows = [outflow_of(doc_col, doc_row, rates[h]) for h in range(LOCAL)]
    mine = rates[position(lax.axis_index("seq") // (GROUPS * MEMBERS) * MEMBERS) // MEMBERS * LOCAL // ROWS]
    for i, blocks in enumerate((1, MEMBERS, 2 * MEMBERS)):
        fades[i : i + 1, :] = jnp.exp(jnp.full((1, BLOCK), -1.0 * BLOCK * blocks, f32) * mine)
    for copy in copies[2:]:
        copy.wait()
    for h in range(LOCAL):
        key_out = (key[:, head(h)].astype(f32) * outflows[h]).astype(bf16)
        state = dot(key_out, value[:, head(h)], 0, 0)
        for i in range(OWNERS // LOCAL):
            start = (h * OWNERS // LOCAL + i) * SENT
            out[start : start + PIECE, :] = state[i * PIECE : (i + 1) * PIECE]
            out[start + PIECE : start + SENT, :] = doc_row


def intra_kernel(
    rates, docs, gain, query, key, value, grad, weights, attended, scaled, query_in, inflows, outflows
):
    doc_col, doc_row = docs_of(docs)
    scaled[...] = gain[...] * grad[...].astype(f32)
    for h in range(LOCAL):
        scores = dot(query[:, head(h)], key[:, head(h)], 1, 1)
        low = (scores * decays_of(doc_col, doc_row, rates[h])).astype(bf16)
        weights[h] = low
        attended[:, head(h)] = dot(low, value[:, head(h)], 1, 0)
        inflow = inflow_of(doc_col, doc_row, rates[h])
        inflows[h] = inflow
        query_in[:, head(h)] = (query[:, head(h)].astype(f32) * inflow).astype(bf16)
        outflows[h] = outflow_of(doc_col, doc_row, rates[h])


def attend_kernel(inflow, query, scaled, intra, states, attended, sums):
    squares = jnp.zeros((BLOCK, BLOCK), f32)
    crosses = jnp.zeros((BLOCK, BLOCK), f32)
    for h in range(LOCAL):
        low = get_pieces(states, h).astype(bf16)
        whole = intra[:, head(h)] + inflow[h] * dot(query[:, head(h)], low, 1, 0)
        attended[:, head(h)] = whole
        squares = squares + whole * whole
        crosses = crosses + scaled[:, head(h)] * whole
    square_row = jnp.sum(squares.T, axis=0, keepdims=True)
    cross_row = jnp.sum(crosses.T, axis=0, keepdims=True)
    for i in range(sums.shape[0]):
        sums[i, 0:1, :] = square_row
        sums[i, 1:2, :] = cross_row


def grad_kernel(query_in, scaled, attended, sums, low_grad, out):
    both = jnp.sum(sums[...], axis=0)
    width = HEADS * HEAD_DIM
    inv_rms = lax.rsqrt(both[0:1] / width + epsilon)
    slope = both[1:2] * (inv_rms * inv_rms * inv_rms) / width
    inv_col, slope_col = square(inv_rms).T, square(slope).T
    for h in range(LOCAL):
        low = (scaled[:, head(h)] * inv_col - attended[:, head(h)] * slope_col).astype(bf16)
        low_grad[:, head(h)] = low
        put_pieces(out, h, dot(query_in[:, head(h)], low, 0, 0))


def back_intra_kernel(
    rates, docs, inflow, query, key, value, weights, low_grad, states, query_grad, key_part, value_part
):
    doc_col, doc_row = docs_of(docs)
    for h in range(LOCAL):
        low = low_grad[:, head(h)]
        scores = dot(low, value[:, head(h)], 1, 1)
        grad_weights = (scores * decays_of(doc_col, doc_row, rates[h])).astype(bf16)
        state = get_pieces(states, h).astype(bf16)
        whole = dot(grad_weights, key[:, head(h)], 1, 0) + inflow[h] * dot(low, state, 1, 1)
        query_grad[:, head(h)] = whole.astype(bf16)
        key_part[:, head(h)] = dot(grad_weights, query[:, head(h)], 0, 0)
        value_part[:, head(h)] = dot(weights[h], low, 0, 0)


def finish_kernel(outflow, key, value, key_part, value_part, states, key_grad, value_grad):
    for h in range(LOCAL):
        low = get_pieces(states, h).astype(bf16)
        more = outflow[h] * dot(value[:, head(h)], low, 1, 1)
        key_grad[:, head(h)] = (key_part[:, head(h)] + more).astype(bf16)
        more = outflow[h] * dot(key[:, head(h)], low, 1, 0)
        value_grad[:, head(h)] = (value_part[:, head(h)] + more).astype(bf16)


def place():
    group, odd = (lax.axis_index("seq") // MEMBERS) % GROUPS, (lax.axis_index("head") + 1) % 2
    turn = (group + odd) % GROUPS
    return turn, odd == 1, (odd == 1) & (turn == 0), (odd == 1) & (turn == 1)


def passing(same, fade):
    return jnp.where(same, fade, 0.0)


def flipped():
    return lax.axis_index("head") % 2 == 1


def position(block):
    return jnp.where(flipped(), block ^ FLIPS[1], block ^ FLIPS[0])


def slot(x, i):
    return position(x * MEMBERS + i)


def rows_of(pieces, x, i, first, count):
    start = ((x * MEMBERS + i) ^ FLIPS[0]) * SENT + first
    other = ((x * MEMBERS + i) ^ FLIPS[1]) * SENT + first
    return jnp.where(flipped(), pieces[other : other + count, :], pieces[start : start + count, :])


def first_doc(pieces, x, i):
    return jnp.broadcast_to(rows_of(pieces, x, i, PIECE, 1)[:, 0:1], (1, BLOCK))


def last_doc(pieces, x, i):
    return jnp.broadcast_to(rows_of(pieces, x, i, PIECE, 1)[:, BLOCK - 1 :], (1, BLOCK))


def piece_of(pieces, x, i):
    return rows_of(pieces, x, i, 0, PIECE)


def state_of(total, x):
    return total[x * PIECE : (x + 1) * PIECE, :]


def doc_of(total, x):
    return total[DOC + x : DOC + x + 1, :]


def pick(read, total, x, late, empty):
    soon = read(total, x) if x < ROWS else empty
    return jnp.where(late, read(total, x - 1) if x else empty, soon)


def state_at(total, x, late):
    return pick(state_of, total, x, late, jnp.zeros((PIECE, BLOCK), f32))


def doc_at(total, x, late):
    return pick(doc_of, total, x, late, -jnp.ones((1, BLOCK), f32))


def ordered(first, mine, theirs):
    return jnp.where(first, mine, theirs), jnp.where(first, theirs, mine)


def group_total_kernel(fades, pieces, out):
    fade = fades[0:1, :]
    out[DOC:, :] = jnp.zeros((TALL - DOC, BLOCK), f32)
    for x in range(ROWS):
        total = piece_of(pieces, x, 0)
        for i in range(1, MEMBERS):
            same = last_doc(pieces, x, i) == last_doc(pieces, x, i - 1)
            total = passing(same, fade) * total + piece_of(pieces, x, i)
        out[x * PIECE : (x + 1) * PIECE, :] = total
        out[DOC + x : DOC + x + 1, :] = last_doc(pieces, x, MEMBERS - 1)


def pair_total_kernel(fades, mine, theirs, out):
    turn, _, late, partner_late = place()
    first, fade = turn % 2 == 0, fades[1:2, :]
    out[DOC:, :] = jnp.zeros((TALL - DOC, BLOCK), f32)
    for x in range(ROWS):
        low_doc, high_doc = ordered(first, doc_at(mine, x, late), doc_at(theirs, x, partner_late))
        low, high = ordered(first, state_at(mine, x, late), state_at(theirs, x, partner_late))
        out[x * PIECE : (x + 1) * PIECE, :] = passing(low_doc == high_doc, fade) * low + high
        out[DOC + x : DOC + x + 1, :] = high_doc


def row_docs(mine, theirs, turn, x):
    return ordered(turn < 2, doc_of(mine, x), doc_of(theirs, x))


def before_row(mine, theirs, turn, x):
    return row_docs(mine, theirs, turn, x - 1)[1] if x else -jnp.ones((1, BLOCK), f32)


def before_pair(mine, theirs, turn, x):
    before = before_row(mine, theirs, turn, x)
    return jnp.where(turn > 1, row_docs(mine, theirs, turn, x)[0], before) if x < ROWS else before


def before_group(partner, mine, theirs, x):
    turn, _, _, partner_late = place()
    before = before_pair(mine, theirs, turn, x)
    return jnp.where(turn % 2 == 1, doc_at(partner, x, partner_late), before) if x < ROWS else before


def states_kernel(fades, pieces, partner, mine, theirs, out):
    turn, _, late, partner_late = place()
    one, four, eight = fades[0:1, :], fades[1:2, :], fades[2:3, :]
    carry = jnp.zeros((PIECE, BLOCK), f32)
    entries = []
    for x in range(ROWS):
        low_doc, high_doc = row_docs(mine, theirs, turn, x)
        low, high = ordered(turn < 2, state_of(mine, x), state_of(theirs, x))
        half = passing(low_doc == before_row(mine, theirs, turn, x), eight) * carry + low
        state = jnp.where(turn > 1, half, carry)
        same = doc_at(partner, x, partner_late) == before_pair(mine, theirs, turn, x)
        longer = passing(same, four) * state + state_at(partner, x, partner_late)
        entries.append(jnp.where(turn % 2 == 1, longer, state))
        carry = passing(high_doc == low_doc, eight) * half + high
    entries.append(carry)
    docs = [before_group(partner, mine, theirs, x) for x in range(ROWS + 1)]
    for x in range(ROWS):
        state = jnp.where(late, entries[x + 1], entries[x])
        prev = jnp.where(late, docs[x + 1], docs[x])
        for i in range(MEMBERS):
            out[slot(x, i)] = passing(first_doc(pieces, x, i) == prev, 1.0) * state
            last = last_doc(pieces, x, i)
            if i < MEMBERS - 1:
                state = passing(last == prev, one) * state + piece_of(pieces, x, i)
            prev = last


def back_total_kernel(fades, pieces, partner, mine, theirs, grads, out):
    late, fade = place()[2], fades[0:1, :]
    docs = [before_group(partner, mine, theirs, x) for x in range(ROWS + 1)]
    for x in range(ROWS):
        prev = jnp.where(late, docs[x + 1], docs[x])
        total = jnp.zeros((PIECE, BLOCK), f32)
        for i in range(MEMBERS - 1, -1, -1):
            older = last_doc(pieces, x, i - 1) if i else prev
            local = passing(first_doc(pieces, x, i) == older, 1.0) * grads[slot(x, i)]
            total = passing(last_doc(pieces, x, i) == older, fade) * total + local
        out[x * PIECE : (x + 1) * PIECE, :] = total


def back_pair_kernel(fades, total, partner, mine, theirs, grad, grad_theirs, out):
    turn, odd, late, partner_late = place()
    first, fade = turn % 2 == 0, fades[1:2, :]
    pairs = []
    for x in range(ROWS + 1):
        low_doc = jnp.where(first, doc_at(total, x, late), doc_at(partner, x, partner_late))
        low, high = ordered(first, state_at(grad, x, late), state_at(grad_theirs, x, partner_late))
        same = low_doc == before_pair(mine, theirs, turn, x)
        pairs.append(low + passing(same, fade) * high)
    for x in range(ROWS):
        out[x * PIECE : (x + 1) * PIECE, :] = jnp.where(odd & (turn < 2), pairs[x + 1], pairs[x])


def back_states_kernel(
    fades, pieces, total, partner, mine, theirs, grads, partner_grad, pair_grad, other_grad, out
):
    turn, odd, late, partner_late = place()
    one, four, eight = fades[0:1, :], fades[1:2, :], fades[2:3, :]

    def low_grad(x):
        return jnp.where(turn < 2, state_at(pair_grad, x, odd), state_at(other_grad, x, odd))

    carry = low_grad(ROWS)
    entries = [jnp.zeros((PIECE, BLOCK), f32)]
    for x in range(ROWS - 1, -1, -1):
        low_doc, high_doc = row_docs(mine, theirs, turn, x)
        high = jnp.where(turn < 2, state_of(other_grad, x), state_of(pair_grad, x))
        half = high + passing(high_doc == low_doc, eight) * carry
        state = jnp.where(turn < 2, half, carry)
        same = doc_at(total, x, late) == doc_at(partner, x, partner_late)
        longer = state_at(partner_grad, x, partner_late) + passing(same, four) * state
        entries.insert(0, jnp.where(turn % 2 == 0, longer, state))
        carry = low_grad(x) + passing(low_doc == before_row(mine, theirs, turn, x), eight) * half
    for x in range(ROWS):
        state = jnp.where(late, entries[x + 1], entries[x])
        for i in range(MEMBERS - 1, -1, -1):
            out[slot(x, i)] = state
            if i:
                last, older = last_doc(pieces, x, i), last_doc(pieces, x, i - 1)
                local = passing(first_doc(pieces, x, i) == older, 1.0) * grads[slot(x, i)]
                state = passing(last == older, one) * state + local


def call(kernel, name, outs, *args, flops=1):
    scalars = args[0].shape == (LOCAL,)
    shapes = [jax.ShapeDtypeStruct(shape, dtype) for shape, dtype in outs]
    moved = sum(a.size * a.dtype.itemsize for a in (*args, *shapes))
    out = pl.pallas_call(
        kernel,
        out_shape=shapes,
        in_specs=[SMEM if scalars else VMEM] + [VMEM] * (len(args) - 1),
        out_specs=[VMEM] * len(shapes),
        name=name,
        compiler_params=pltpu.CompilerParams(vmem_limit_bytes=32 * 1024 * 1024),
        cost_estimate=pl.CostEstimate(flops=flops, bytes_accessed=moved, transcendentals=0),
    )(*args)
    return out[0] if len(out) == 1 else out


def per_device(query, key, value, grad, gain, rates, doc_ids):
    row_len = GROUPS * MEMBERS
    blocks = range(ROWS * row_len)
    owners = [
        [x * row_len + k * MEMBERS + i for x in range(ROWS) for i in range(MEMBERS)] for k in range(GROUPS)
    ]
    heads = lax.axis_size("head")
    orders = [
        [group[j ^ FLIPS[h % 2]] * heads + h for j in range(OWNERS)] for group in owners for h in range(heads)
    ]
    swap = functools.partial(
        lax.all_to_all, axis_name=("seq", "head"), split_axis=0, concat_axis=0, axis_index_groups=orders, tiled=True
    )

    def other_group(total, step):
        pairs = [
            (i * heads + h, (i ^ ((1, 3)[(step + h + 1) % 2] * MEMBERS)) * heads + h)
            for i in blocks
            for h in range(heads)
        ]
        return lax.ppermute(total, ("seq", "head"), pairs)

    docs = doc_ids.reshape(1, BLOCK)
    gain = gain.reshape(1, LOCAL * HEAD_DIM)
    wide = (BLOCK, LOCAL * HEAD_DIM)
    each = (LOCAL, BLOCK, BLOCK)
    cut = (OWNERS, PIECE, HEAD_DIM)
    one = 2 * LOCAL * BLOCK * BLOCK * HEAD_DIM

    local, fades = pl.pallas_call(
        local_state_kernel,
        out_shape=[
            jax.ShapeDtypeStruct((OWNERS * SENT, HEAD_DIM), f32),
            jax.ShapeDtypeStruct((8, BLOCK), f32),
        ],
        in_specs=[pl.BlockSpec(memory_space=pl.ANY)] * 4,
        out_specs=[VMEM] * 2,
        scratch_shapes=[
            pltpu.SMEM((LOCAL,), f32),
            pltpu.VMEM((1, BLOCK), jnp.int32),
            pltpu.VMEM(wide, bf16),
            pltpu.VMEM(wide, bf16),
            pltpu.SemaphoreType.DMA((4,)),
        ],
        name="local_state",
        compiler_params=pltpu.CompilerParams(vmem_limit_bytes=60 * 1024 * 1024),
        cost_estimate=pl.CostEstimate(flops=one, bytes_accessed=1 << 19, transcendentals=0),
    )(rates, docs, key, value)
    pieces = swap(local.reshape(OWNERS, SENT, 1, HEAD_DIM)).reshape(local.shape)
    total = call(group_total_kernel, "group_total", [((TALL, HEAD_DIM), f32)], fades, pieces)
    partner = other_group(total, 0)
    weights, intra, scaled, query_in, inflow, outflow = call(
        intra_kernel, "intra",
        [(each, bf16), (wide, f32), (wide, f32), (wide, bf16), (each, f32), (each, f32)],
        rates, docs, gain, query, key, value, grad, flops=2 * one,
    )
    partner, weights, intra = lax.optimization_barrier((partner, weights, intra))
    pair = call(pair_total_kernel, "pair_total", [((TALL, HEAD_DIM), f32)], fades, total, partner)
    other = other_group(pair, 1)
    states = swap(call(states_kernel, "states", [(cut, f32)], fades, pieces, partner, pair, other))
    attended, sums = call(
        attend_kernel, "attend", [(wide, f32), ((8, 2, BLOCK), f32)],
        inflow, query, scaled, intra, states, flops=one,
    )
    spread = [[0, 3, 4, 7, 2, 1, 6, 5]]
    sums = lax.all_to_all(sums, "head", 0, 0, axis_index_groups=spread, tiled=True)
    low_grad, local_grad = call(
        grad_kernel, "grad", [(wide, bf16), (cut, f32)],
        query_in, scaled, attended, sums, flops=one,
    )
    grads = swap(local_grad)
    total_grad = call(
        back_total_kernel, "back_total", [((DOC, HEAD_DIM), f32)], fades, pieces, partner, pair, other, grads
    )
    partner_grad = other_group(total_grad, 0)
    query_grad, key_part, value_part = call(
        back_intra_kernel, "back_intra", [(wide, bf16), (wide, f32), (wide, f32)],
        rates, docs, inflow, query, key, value, weights, low_grad, states, flops=5 * one,
    )
    partner_grad, key_part, value_part = lax.optimization_barrier((partner_grad, key_part, value_part))
    pair_grad = call(
        back_pair_kernel, "back_pair", [((DOC, HEAD_DIM), f32)],
        fades, total, partner, pair, other, total_grad, partner_grad,
    )
    other_grad = other_group(pair_grad, 1)
    states_out = call(
        back_states_kernel, "back_states", [(cut, f32)],
        fades, pieces, total, partner, pair, other, grads, partner_grad, pair_grad, other_grad,
    )
    states_out = swap(states_out)
    key_grad, value_grad = call(
        finish_kernel, "finish", [(wide, bf16), (wide, bf16)],
        outflow, key, value, key_part, value_part, states_out, flops=2 * one,
    )
    return query_grad, key_grad, value_grad


def solution(mesh):
    return jax.shard_map(
        per_device,
        mesh=mesh,
        in_specs=(
            P("seq", "head"),
            P("seq", "head"),
            P("seq", "head"),
            P("seq", "head"),
            P("head"),
            P("head"),
            P("seq"),
        ),
        out_specs=(P("seq", "head"), P("seq", "head"), P("seq", "head")),
        check_vma=False,
    )
```

```python
import functools

import jax
import jax.numpy as jnp
from jax import lax
from jax.experimental import pallas as pl
from jax.experimental.pallas import tpu as pltpu
from jax.sharding import PartitionSpec as P

HEADS = 32
HEAD_DIM = 128
BLOCK = 128
LOCAL = 4
MEMBERS = 4
GROUPS = 4
ROWS = 4
OWNERS = ROWS * MEMBERS
FLIPS = (10, 15)
PIECE = LOCAL * HEAD_DIM // OWNERS
SENT = PIECE + 1
DOC = ROWS * PIECE
TALL = DOC + 8

epsilon = 1e-06
f32 = jnp.float32
bf16 = jnp.bfloat16

VMEM = pl.BlockSpec(memory_space=pltpu.VMEM)
SMEM = pl.BlockSpec(memory_space=pltpu.SMEM)


def dot(a, b, a_dim, b_dim):
    return lax.dot_general(a, b, (((a_dim,), (b_dim,)), ((), ())), preferred_element_type=f32)


def square(row):
    return jnp.broadcast_to(row, (BLOCK, BLOCK))


def iota(axis):
    return lax.broadcasted_iota(jnp.int32, (BLOCK, BLOCK), axis).astype(f32)


def head(h):
    return slice(h * HEAD_DIM, (h + 1) * HEAD_DIM)


def outflow_of(doc_col, doc_row, rate):
    last = doc_row[:, BLOCK - 1 :]
    return jnp.where(doc_col == last, jnp.exp(-rate * (BLOCK - 1.0 - iota(0))), 0.0)


def inflow_of(doc_col, doc_row, rate):
    return jnp.where(doc_col == doc_row[:, 0:1], jnp.exp(-rate * (iota(0) + 1.0)), 0.0)


def decays_of(doc_col, doc_row, rate):
    offset = iota(0) - iota(1)
    inside = (offset >= 0.0) & (doc_col == doc_row)
    return jnp.where(inside, jnp.exp(-rate * jnp.maximum(offset, 0.0)), 0.0)


def docs_of(docs):
    row = docs[...].astype(f32)
    return square(row).T, row


def put_pieces(out, h, matrix):
    each = OWNERS // LOCAL
    for i in range(each):
        out[h * each + i] = matrix[i * PIECE : (i + 1) * PIECE]


def get_pieces(pieces, h):
    each = OWNERS // LOCAL
    return jnp.concatenate([pieces[h * each + i] for i in range(each)], axis=0)


def local_state_kernel(
    rates_in, docs_in, key_in, value_in, out, fades, rates, docs, key, value, sems
):
    pairs = ((rates_in, rates), (docs_in, docs), (key_in, key), (value_in, value))
    copies = [pltpu.make_async_copy(a, b, sems.at[i]) for i, (a, b) in enumerate(pairs)]
    for copy in copies:
        copy.start()
    for copy in copies[:2]:
        copy.wait()
    doc_col, doc_row = docs_of(docs)
    outflows = [outflow_of(doc_col, doc_row, rates[h]) for h in range(LOCAL)]
    mine = rates[position(lax.axis_index("seq") // (GROUPS * MEMBERS) * MEMBERS) // MEMBERS * LOCAL // ROWS]
    for i, blocks in enumerate((1, MEMBERS, 2 * MEMBERS)):
        fades[i : i + 1, :] = jnp.exp(jnp.full((1, BLOCK), -1.0 * BLOCK * blocks, f32) * mine)
    for copy in copies[2:]:
        copy.wait()
    for h in range(LOCAL):
        key_out = (key[:, head(h)].astype(f32) * outflows[h]).astype(bf16)
        state = dot(key_out, value[:, head(h)], 0, 0)
        for i in range(OWNERS // LOCAL):
            start = (h * OWNERS // LOCAL + i) * SENT
            out[start : start + PIECE, :] = state[i * PIECE : (i + 1) * PIECE]
            out[start + PIECE : start + SENT, :] = doc_row


def intra_kernel(
    rates, docs, gain, query, key, value, grad, weights, attended, scaled, query_in, inflows, outflows
):
    doc_col, doc_row = docs_of(docs)
    scaled[...] = gain[...] * grad[...].astype(f32)
    for h in range(LOCAL):
        scores = dot(query[:, head(h)], key[:, head(h)], 1, 1)
        low = (scores * decays_of(doc_col, doc_row, rates[h])).astype(bf16)
        weights[h] = low
        attended[:, head(h)] = dot(low, value[:, head(h)], 1, 0)
        inflow = inflow_of(doc_col, doc_row, rates[h])
        inflows[h] = inflow
        query_in[:, head(h)] = (query[:, head(h)].astype(f32) * inflow).astype(bf16)
        outflows[h] = outflow_of(doc_col, doc_row, rates[h])


def attend_kernel(inflow, query, scaled, intra, states, attended, sums):
    squares = jnp.zeros((BLOCK, BLOCK), f32)
    crosses = jnp.zeros((BLOCK, BLOCK), f32)
    for h in range(LOCAL):
        low = get_pieces(states, h).astype(bf16)
        whole = intra[:, head(h)] + inflow[h] * dot(query[:, head(h)], low, 1, 0)
        attended[:, head(h)] = whole
        squares = squares + whole * whole
        crosses = crosses + scaled[:, head(h)] * whole
    square_row = jnp.sum(squares.T, axis=0, keepdims=True)
    cross_row = jnp.sum(crosses.T, axis=0, keepdims=True)
    for i in range(sums.shape[0]):
        sums[i, 0:1, :] = square_row
        sums[i, 1:2, :] = cross_row


def grad_kernel(query_in, scaled, attended, sums, low_grad, out):
    both = jnp.sum(sums[...], axis=0)
    width = HEADS * HEAD_DIM
    inv_rms = lax.rsqrt(both[0:1] / width + epsilon)
    slope = both[1:2] * (inv_rms * inv_rms * inv_rms) / width
    inv_col, slope_col = square(inv_rms).T, square(slope).T
    for h in range(LOCAL):
        low = (scaled[:, head(h)] * inv_col - attended[:, head(h)] * slope_col).astype(bf16)
        low_grad[:, head(h)] = low
        put_pieces(out, h, dot(query_in[:, head(h)], low, 0, 0))


def back_intra_kernel(
    rates, docs, inflow, query, key, value, weights, low_grad, states, query_grad, key_part, value_part
):
    doc_col, doc_row = docs_of(docs)
    for h in range(LOCAL):
        low = low_grad[:, head(h)]
        scores = dot(low, value[:, head(h)], 1, 1)
        grad_weights = (scores * decays_of(doc_col, doc_row, rates[h])).astype(bf16)
        state = get_pieces(states, h).astype(bf16)
        whole = dot(grad_weights, key[:, head(h)], 1, 0) + inflow[h] * dot(low, state, 1, 1)
        query_grad[:, head(h)] = whole.astype(bf16)
        key_part[:, head(h)] = dot(grad_weights, query[:, head(h)], 0, 0)
        value_part[:, head(h)] = dot(weights[h], low, 0, 0)


def finish_kernel(outflow, key, value, key_part, value_part, states, key_grad, value_grad):
    for h in range(LOCAL):
        low = get_pieces(states, h).astype(bf16)
        more = outflow[h] * dot(value[:, head(h)], low, 1, 1)
        key_grad[:, head(h)] = (key_part[:, head(h)] + more).astype(bf16)
        more = outflow[h] * dot(key[:, head(h)], low, 1, 0)
        value_grad[:, head(h)] = (value_part[:, head(h)] + more).astype(bf16)


def place():
    group, odd = (lax.axis_index("seq") // MEMBERS) % GROUPS, (lax.axis_index("head") + 1) % 2
    turn = (group + odd) % GROUPS
    return turn, odd == 1, (odd == 1) & (turn == 0), (odd == 1) & (turn == 1)


def passing(same, fade):
    return jnp.where(same, fade, 0.0)


def flipped():
    return lax.axis_index("head") % 2 == 1


def position(block):
    return jnp.where(flipped(), block ^ FLIPS[1], block ^ FLIPS[0])


def slot(x, i):
    return position(x * MEMBERS + i)


def rows_of(pieces, x, i, first, count):
    start = ((x * MEMBERS + i) ^ FLIPS[0]) * SENT + first
    other = ((x * MEMBERS + i) ^ FLIPS[1]) * SENT + first
    return jnp.where(flipped(), pieces[other : other + count, :], pieces[start : start + count, :])


def first_doc(pieces, x, i):
    return jnp.broadcast_to(rows_of(pieces, x, i, PIECE, 1)[:, 0:1], (1, BLOCK))


def last_doc(pieces, x, i):
    return jnp.broadcast_to(rows_of(pieces, x, i, PIECE, 1)[:, BLOCK - 1 :], (1, BLOCK))


def piece_of(pieces, x, i):
    return rows_of(pieces, x, i, 0, PIECE)


def state_of(total, x):
    return total[x * PIECE : (x + 1) * PIECE, :]


def doc_of(total, x):
    return total[DOC + x : DOC + x + 1, :]


def pick(read, total, x, late, empty):
    soon = read(total, x) if x < ROWS else empty
    return jnp.where(late, read(total, x - 1) if x else empty, soon)


def state_at(total, x, late):
    return pick(state_of, total, x, late, jnp.zeros((PIECE, BLOCK), f32))


def doc_at(total, x, late):
    return pick(doc_of, total, x, late, -jnp.ones((1, BLOCK), f32))


def ordered(first, mine, theirs):
    return jnp.where(first, mine, theirs), jnp.where(first, theirs, mine)


def group_total_kernel(fades, pieces, out):
    fade = fades[0:1, :]
    out[DOC:, :] = jnp.zeros((TALL - DOC, BLOCK), f32)
    for x in range(ROWS):
        total = piece_of(pieces, x, 0)
        for i in range(1, MEMBERS):
            same = last_doc(pieces, x, i) == last_doc(pieces, x, i - 1)
            total = passing(same, fade) * total + piece_of(pieces, x, i)
        out[x * PIECE : (x + 1) * PIECE, :] = total
        out[DOC + x : DOC + x + 1, :] = last_doc(pieces, x, MEMBERS - 1)


def pair_total_kernel(fades, mine, theirs, out):
    turn, _, late, partner_late = place()
    first, fade = turn % 2 == 0, fades[1:2, :]
    out[DOC:, :] = jnp.zeros((TALL - DOC, BLOCK), f32)
    for x in range(ROWS):
        low_doc, high_doc = ordered(first, doc_at(mine, x, late), doc_at(theirs, x, partner_late))
        low, high = ordered(first, state_at(mine, x, late), state_at(theirs, x, partner_late))
        out[x * PIECE : (x + 1) * PIECE, :] = passing(low_doc == high_doc, fade) * low + high
        out[DOC + x : DOC + x + 1, :] = high_doc


def row_docs(mine, theirs, turn, x):
    return ordered(turn < 2, doc_of(mine, x), doc_of(theirs, x))


def before_row(mine, theirs, turn, x):
    return row_docs(mine, theirs, turn, x - 1)[1] if x else -jnp.ones((1, BLOCK), f32)


def before_pair(mine, theirs, turn, x):
    before = before_row(mine, theirs, turn, x)
    return jnp.where(turn > 1, row_docs(mine, theirs, turn, x)[0], before) if x < ROWS else before


def before_group(partner, mine, theirs, x):
    turn, _, _, partner_late = place()
    before = before_pair(mine, theirs, turn, x)
    return jnp.where(turn % 2 == 1, doc_at(partner, x, partner_late), before) if x < ROWS else before


def states_kernel(fades, pieces, partner, mine, theirs, out):
    turn, _, late, partner_late = place()
    one, four, eight = fades[0:1, :], fades[1:2, :], fades[2:3, :]
    carry = jnp.zeros((PIECE, BLOCK), f32)
    entries = []
    for x in range(ROWS):
        low_doc, high_doc = row_docs(mine, theirs, turn, x)
        low, high = ordered(turn < 2, state_of(mine, x), state_of(theirs, x))
        half = passing(low_doc == before_row(mine, theirs, turn, x), eight) * carry + low
        state = jnp.where(turn > 1, half, carry)
        same = doc_at(partner, x, partner_late) == before_pair(mine, theirs, turn, x)
        longer = passing(same, four) * state + state_at(partner, x, partner_late)
        entries.append(jnp.where(turn % 2 == 1, longer, state))
        carry = passing(high_doc == low_doc, eight) * half + high
    entries.append(carry)
    docs = [before_group(partner, mine, theirs, x) for x in range(ROWS + 1)]
    for x in range(ROWS):
        state = jnp.where(late, entries[x + 1], entries[x])
        prev = jnp.where(late, docs[x + 1], docs[x])
        for i in range(MEMBERS):
            out[slot(x, i)] = passing(first_doc(pieces, x, i) == prev, 1.0) * state
            last = last_doc(pieces, x, i)
            if i < MEMBERS - 1:
                state = passing(last == prev, one) * state + piece_of(pieces, x, i)
            prev = last


def back_total_kernel(fades, pieces, partner, mine, theirs, grads, out):
    late, fade = place()[2], fades[0:1, :]
    docs = [before_group(partner, mine, theirs, x) for x in range(ROWS + 1)]
    for x in range(ROWS):
        prev = jnp.where(late, docs[x + 1], docs[x])
        total = jnp.zeros((PIECE, BLOCK), f32)
        for i in range(MEMBERS - 1, -1, -1):
            older = last_doc(pieces, x, i - 1) if i else prev
            local = passing(first_doc(pieces, x, i) == older, 1.0) * grads[slot(x, i)]
            total = passing(last_doc(pieces, x, i) == older, fade) * total + local
        out[x * PIECE : (x + 1) * PIECE, :] = total


def back_pair_kernel(fades, total, partner, mine, theirs, grad, grad_theirs, out):
    turn, odd, late, partner_late = place()
    first, fade = turn % 2 == 0, fades[1:2, :]
    pairs = []
    for x in range(ROWS + 1):
        low_doc = jnp.where(first, doc_at(total, x, late), doc_at(partner, x, partner_late))
        low, high = ordered(first, state_at(grad, x, late), state_at(grad_theirs, x, partner_late))
        same = low_doc == before_pair(mine, theirs, turn, x)
        pairs.append(low + passing(same, fade) * high)
    for x in range(ROWS):
        out[x * PIECE : (x + 1) * PIECE, :] = jnp.where(odd & (turn < 2), pairs[x + 1], pairs[x])


def back_states_kernel(
    fades, pieces, total, partner, mine, theirs, grads, partner_grad, pair_grad, other_grad, out
):
    turn, odd, late, partner_late = place()
    one, four, eight = fades[0:1, :], fades[1:2, :], fades[2:3, :]

    def low_grad(x):
        return jnp.where(turn < 2, state_at(pair_grad, x, odd), state_at(other_grad, x, odd))

    carry = low_grad(ROWS)
    entries = [jnp.zeros((PIECE, BLOCK), f32)]
    for x in range(ROWS - 1, -1, -1):
        low_doc, high_doc = row_docs(mine, theirs, turn, x)
        high = jnp.where(turn < 2, state_of(other_grad, x), state_of(pair_grad, x))
        half = high + passing(high_doc == low_doc, eight) * carry
        state = jnp.where(turn < 2, half, carry)
        same = doc_at(total, x, late) == doc_at(partner, x, partner_late)
        longer = state_at(partner_grad, x, partner_late) + passing(same, four) * state
        entries.insert(0, jnp.where(turn % 2 == 0, longer, state))
        carry = low_grad(x) + passing(low_doc == before_row(mine, theirs, turn, x), eight) * half
    for x in range(ROWS):
        state = jnp.where(late, entries[x + 1], entries[x])
        for i in range(MEMBERS - 1, -1, -1):
            out[slot(x, i)] = state
            if i:
                last, older = last_doc(pieces, x, i), last_doc(pieces, x, i - 1)
                local = passing(first_doc(pieces, x, i) == older, 1.0) * grads[slot(x, i)]
                state = passing(last == older, one) * state + local


def call(kernel, name, outs, *args, flops=1):
    scalars = args[0].shape == (LOCAL,)
    shapes = [jax.ShapeDtypeStruct(shape, dtype) for shape, dtype in outs]
    moved = sum(a.size * a.dtype.itemsize for a in (*args, *shapes))
    out = pl.pallas_call(
        kernel,
        out_shape=shapes,
        in_specs=[SMEM if scalars else VMEM] + [VMEM] * (len(args) - 1),
        out_specs=[VMEM] * len(shapes),
        name=name,
        compiler_params=pltpu.CompilerParams(vmem_limit_bytes=32 * 1024 * 1024),
        cost_estimate=pl.CostEstimate(flops=flops, bytes_accessed=moved, transcendentals=0),
    )(*args)
    return out[0] if len(out) == 1 else out


def per_device(query, key, value, grad, gain, rates, doc_ids):
    row_len = GROUPS * MEMBERS
    blocks = range(ROWS * row_len)
    owners = [
        [x * row_len + k * MEMBERS + i for x in range(ROWS) for i in range(MEMBERS)] for k in range(GROUPS)
    ]
    heads = lax.axis_size("head")
    orders = [
        [group[j ^ FLIPS[h % 2]] * heads + h for j in range(OWNERS)] for group in owners for h in range(heads)
    ]
    swap = functools.partial(
        lax.all_to_all, axis_name=("seq", "head"), split_axis=0, concat_axis=0, axis_index_groups=orders, tiled=True
    )

    def other_group(total, step):
        pairs = [
            (i * heads + h, (i ^ ((1, 3)[(step + h + 1) % 2] * MEMBERS)) * heads + h)
            for i in blocks
            for h in range(heads)
        ]
        return lax.ppermute(total, ("seq", "head"), pairs)

    docs = doc_ids.reshape(1, BLOCK)
    gain = gain.reshape(1, LOCAL * HEAD_DIM)
    wide = (BLOCK, LOCAL * HEAD_DIM)
    each = (LOCAL, BLOCK, BLOCK)
    cut = (OWNERS, PIECE, HEAD_DIM)
    one = 2 * LOCAL * BLOCK * BLOCK * HEAD_DIM

    local, fades = pl.pallas_call(
        local_state_kernel,
        out_shape=[
            jax.ShapeDtypeStruct((OWNERS * SENT, HEAD_DIM), f32),
            jax.ShapeDtypeStruct((8, BLOCK), f32),
        ],
        in_specs=[pl.BlockSpec(memory_space=pl.ANY)] * 4,
        out_specs=[VMEM] * 2,
        scratch_shapes=[
            pltpu.SMEM((LOCAL,), f32),
            pltpu.VMEM((1, BLOCK), jnp.int32),
            pltpu.VMEM(wide, bf16),
            pltpu.VMEM(wide, bf16),
            pltpu.SemaphoreType.DMA((4,)),
        ],
        name="local_state",
        compiler_params=pltpu.CompilerParams(vmem_limit_bytes=60 * 1024 * 1024),
        cost_estimate=pl.CostEstimate(flops=one, bytes_accessed=1 << 19, transcendentals=0),
    )(rates, docs, key, value)
    pieces = swap(local.reshape(OWNERS, SENT, 1, HEAD_DIM)).reshape(local.shape)
    total = call(group_total_kernel, "group_total", [((TALL, HEAD_DIM), f32)], fades, pieces)
    partner = other_group(total, 0)
    weights, intra, scaled, query_in, inflow, outflow = call(
        intra_kernel, "intra",
        [(each, bf16), (wide, f32), (wide, f32), (wide, bf16), (each, f32), (each, f32)],
        rates, docs, gain, query, key, value, grad, flops=2 * one,
    )
    partner, weights, intra = lax.optimization_barrier((partner, weights, intra))
    pair = call(pair_total_kernel, "pair_total", [((TALL, HEAD_DIM), f32)], fades, total, partner)
    other = other_group(pair, 1)
    states = swap(call(states_kernel, "states", [(cut, f32)], fades, pieces, partner, pair, other))
    attended, sums = call(
        attend_kernel, "attend", [(wide, f32), ((8, 2, BLOCK), f32)],
        inflow, query, scaled, intra, states, flops=one,
    )
    spread = [[0, 3, 4, 7, 2, 1, 6, 5]]
    sums = lax.all_to_all(sums, "head", 0, 0, axis_index_groups=spread, tiled=True)
    low_grad, local_grad = call(
        grad_kernel, "grad", [(wide, bf16), (cut, f32)],
        query_in, scaled, attended, sums, flops=one,
    )
    grads = swap(local_grad)
    total_grad = call(
        back_total_kernel, "back_total", [((DOC, HEAD_DIM), f32)], fades, pieces, partner, pair, other, grads
    )
    partner_grad = other_group(total_grad, 0)
    query_grad, key_part, value_part = call(
        back_intra_kernel, "back_intra", [(wide, bf16), (wide, f32), (wide, f32)],
        rates, docs, inflow, query, key, value, weights, low_grad, states, flops=5 * one,
    )
    pair_grad = call(
        back_pair_kernel, "back_pair", [((DOC, HEAD_DIM), f32)],
        fades, total, partner, pair, other, total_grad, partner_grad,
    )
    other_grad = other_group(pair_grad, 1)
    other_grad, key_part, value_part = lax.optimization_barrier((other_grad, key_part, value_part))
    states_out = call(
        back_states_kernel, "back_states", [(cut, f32)],
        fades, pieces, total, partner, pair, other, grads, partner_grad, pair_grad, other_grad,
    )
    states_out = swap(states_out)
    key_grad, value_grad = call(
        finish_kernel, "finish", [(wide, bf16), (wide, bf16)],
        outflow, key, value, key_part, value_part, states_out, flops=2 * one,
    )
    return query_grad, key_grad, value_grad


def solution(mesh):
    return jax.shard_map(
        per_device,
        mesh=mesh,
        in_specs=(
            P("seq", "head"),
            P("seq", "head"),
            P("seq", "head"),
            P("seq", "head"),
            P("head"),
            P("head"),
            P("seq"),
        ),
        out_specs=(P("seq", "head"), P("seq", "head"), P("seq", "head")),
        check_vma=False,
    )
```
